128 devices in a mesh: obj: 8 (over y, core), scan: 16 (over z, x).
Axes of the slice: x: 4, y: 4, z: 4, core: 2. Of those that a mesh axis runs over, the one named last changes fastest.
Arguments:
- object_field: float32 [2, 4096, 8192], P(None, 'obj', 'scan'), may hold values from -6 to 6
- probe: float32 [2, 256, 256], replicated, may hold values from -3 to 3
- amplitudes: bfloat16 [8, 512, 256, 256], P('obj', 'scan'), may hold values from 0.25 to 2
- corner_row: int32 [8, 256, 2], P('obj', 'scan'), may hold values from -1 to 511, as said below
- corner_col: int32 [8, 256, 2], P('obj', 'scan'), may hold values from -1 to 511, as said below
Outputs:
- object_grad: float32 [2, 4096, 8192], P(None, 'obj', 'scan')
- probe_grad: float32 [16, 2, 256, 256], P('scan')
The draws below stay inside these ranges and needn't reach their ends.
Inputs may be any that keep to these rules, and one draw needn't show every extreme that they name: A slot is live exactly when both corner_row and corner_col are 0 or more; the live slots of each (band, home tile, owner) list come first. In every band some owner has all 2 slots live from every home tile, and some slot is empty. A live position's window lies inside the object. `corner_col`: empty exactly where corner_row is empty.
All inputs are finite; a program needn't handle non-finite values.
Results may differ from the reference program's by a relative error of at most 0.011.
Values may be sent and summed in bfloat16 or wider, within the bound.
A program may use at most 128 MiB of HBM per device.

```python
import math
import jax
import jax.numpy as jnp
from jax import lax

PATCH = 256
TR = 512
TC = 512
CAP = 2
NR = 4096
NC = 8192
N_OBJ = 8
N_SCAN = 16


def route_layout(key):
    count_key = jax.random.fold_in(key, 11)
    busy_key = jax.random.fold_in(key, 12)
    counts = jax.random.randint(count_key, (N_OBJ, N_SCAN, N_SCAN), 0, CAP + 1)
    busy_owner = jax.random.randint(busy_key, (N_OBJ, 1, 1), 0, N_SCAN)
    owner_grid = jnp.arange(N_SCAN, dtype=jnp.int32)[None, None, :]
    home_grid = jnp.arange(N_SCAN, dtype=jnp.int32)[None, :, None]
    counts = jnp.where(owner_grid == busy_owner, CAP, counts)
    counts = jnp.where((home_grid == 0) & (owner_grid == (busy_owner + 1) % N_SCAN), 0, counts)
    slot_grid = jnp.arange(CAP, dtype=jnp.int32)[None, None, None, :]
    live_mask = slot_grid < counts[..., None]
    band_grid = jnp.arange(N_OBJ, dtype=jnp.int32)[:, None, None, None]
    corner_mark = (band_grid == 0) & (home_grid[..., None] == 0) & (owner_grid[..., None] == busy_owner[..., None]) & (slot_grid == 0)
    shape = (N_OBJ, N_SCAN * N_SCAN, CAP)
    return (live_mask.reshape(shape), corner_mark.reshape(shape))


def draw_corner_row(key, part):
    live_mask, corner_mark = route_layout(key)
    key = jax.random.fold_in(key, 1)
    band_grid = jnp.arange(N_OBJ, dtype=jnp.int32)[:, None, None]
    limit = jnp.where(band_grid == N_OBJ - 1, TR - PATCH + 1, TR)
    values = jax.random.randint(key, (N_OBJ, N_SCAN * N_SCAN, CAP), 0, limit)
    values = jnp.where(corner_mark, TR - 1, values)
    return jnp.where(live_mask, values, -1)


def draw_corner_col(key, part):
    live_mask, corner_mark = route_layout(key)
    key = jax.random.fold_in(key, 2)
    home_grid = (jnp.arange(N_SCAN * N_SCAN, dtype=jnp.int32) // N_SCAN)[None, :, None]
    limit = jnp.where(home_grid == N_SCAN - 1, TC - PATCH + 1, TC)
    values = jax.random.randint(key, (N_OBJ, N_SCAN * N_SCAN, CAP), 0, limit)
    values = jnp.where(corner_mark, TC - 1, values)
    return jnp.where(live_mask, values, -1)


def block_scale(own_key, extent, shards, low, top_value):
    def one(axis_at, parts):
        steps = jax.random.uniform(jax.random.fold_in(jax.random.fold_in(own_key, 6), axis_at), (parts,), jnp.float32, low / len(shards), top_value / len(shards))
        return jnp.repeat(jnp.exp(steps), extent[axis_at] // parts).reshape((-1,) + (1,) * (len(extent) - axis_at - 1))

    gain = one(*shards[0])
    for cut in shards[1:]:
        gain = gain * one(*cut)
    return gain


def normal_values(own_key, shape, deviation, most, shards=(), kind=jnp.bfloat16):
    entries = jax.random.normal(own_key, shape, jnp.float32) * deviation
    if len(shards) > 0:
        entries = block_scale(own_key, shape, shards, -0.22, 0.18) * entries
    return jnp.clip(entries, min=-most, max=most).astype(kind)


def setup_inputs(seed: int = 0) -> dict:
    key_list = jax.random.split(jax.random.key(seed), 6)
    return {
        "object_field": normal_values(key_list[0], (2, NR, NC), 1.0, 6.0, ((1, 8), (2, 16)), jnp.float32),
        "probe": normal_values(key_list[1], (2, PATCH, PATCH), 0.5, 3.0, (), jnp.float32),
        "amplitudes": jnp.clip(jnp.exp(math.log(2.0) - 2.0794415 * jax.random.uniform(key_list[2], (N_OBJ, N_SCAN * N_SCAN * CAP, PATCH, PATCH), jnp.float32) ** block_scale(key_list[2], (N_OBJ, N_SCAN * N_SCAN * CAP, PATCH, PATCH), ((0, 8), (1, 16)), -0.2, 0.2)), 0.25, 2.0).astype(jnp.bfloat16),
        "corner_row": draw_corner_row(jax.random.fold_in(key_list[5], 71), 0),
        "corner_col": draw_corner_col(jax.random.fold_in(key_list[5], 71), 0),
    }


def dft_tables(length, direction):
    grid_index = jnp.arange(length, dtype=jnp.int32)
    product = grid_index[:, None] * grid_index[None, :] % length
    phase_angle = 2.0 * math.pi / length * product.astype(jnp.float32)
    norm_scale = 1.0 / math.sqrt(length)
    cos_part = jnp.cos(phase_angle) * norm_scale
    sin_part = direction * jnp.sin(phase_angle) * norm_scale
    left_table = jnp.stack([jnp.stack([cos_part, -sin_part], 1), jnp.stack([sin_part, cos_part], 1)], 0)
    right_table = jnp.stack([jnp.stack([cos_part, sin_part], 1), jnp.stack([-sin_part, cos_part], 1)], 0)
    return (left_table.astype(jnp.bfloat16), right_table.astype(jnp.bfloat16))

def left_apply(table, values):
    return jnp.einsum('cuax,axy->cuy', table.astype(jnp.float32), values.astype(jnp.float32), precision=lax.Precision.HIGHEST)

def right_apply(values, table):
    return jnp.einsum('auy,aycv->cuv', values.astype(jnp.float32), table.astype(jnp.float32), precision=lax.Precision.HIGHEST)

def slot_terms(patch, amplitude, probe, tables):
    fwd_left, fwd_right, inv_left, inv_right = tables
    field = patch.astype(jnp.float32)
    exit_wave = jnp.stack([probe[0] * field[0] - probe[1] * field[1], probe[0] * field[1] + probe[1] * field[0]], 0).astype(jnp.bfloat16)
    half_done = left_apply(fwd_left, exit_wave).astype(jnp.bfloat16)
    far_field = right_apply(half_done, fwd_right)
    magnitude = jnp.sqrt(far_field[0] * far_field[0] + far_field[1] * far_field[1])
    scale_factor = amplitude.astype(jnp.float32) / jnp.maximum(magnitude, 0.1) - 1.0
    difference = (far_field * scale_factor[None]).astype(jnp.bfloat16)
    back_half = left_apply(inv_left, difference).astype(jnp.bfloat16)
    near_field = right_apply(back_half, inv_right)
    object_term = jnp.stack([probe[0] * near_field[0] + probe[1] * near_field[1], probe[0] * near_field[1] - probe[1] * near_field[0]], 0).astype(jnp.bfloat16)
    probe_term = jnp.stack([field[0] * near_field[0] + field[1] * near_field[1], field[0] * near_field[1] - field[1] * near_field[0]], 0)
    return (object_term, probe_term)

def reference(object_field, probe, amplitudes, corner_row, corner_col):
    tables = dft_tables(PATCH, -1.0) + dft_tables(PATCH, 1.0)
    per_band = N_SCAN * N_SCAN * CAP
    flat_rows = corner_row.reshape(-1)
    flat_cols = corner_col.reshape(-1)
    anchor = jnp.zeros((), jnp.int32)

    def visit(state_pair, position):
        band_index = position // per_band
        within = position % per_band
        home_tile = within // (N_SCAN * CAP)
        owner_index = within // CAP % N_SCAN
        slot_index = within % CAP
        row_start = band_index * TR + jnp.maximum(flat_rows[position], 0)
        col_start = home_tile * TC + jnp.maximum(flat_cols[position], 0)
        measured_index = owner_index * (N_SCAN * CAP) + home_tile * CAP + slot_index

        def active(current_pair):
            gradient, probe_sum = current_pair
            patch = lax.dynamic_slice(object_field, (anchor, row_start, col_start), (2, PATCH, PATCH)).astype(jnp.bfloat16)
            amplitude = lax.dynamic_slice(amplitudes, (band_index, measured_index, anchor, anchor), (1, 1, PATCH, PATCH))[0, 0]
            object_term, probe_term = slot_terms(patch, amplitude, probe, tables)
            current = lax.dynamic_slice(gradient, (anchor, row_start, col_start), (2, PATCH, PATCH))
            gradient = lax.dynamic_update_slice(gradient, current + object_term.astype(jnp.float32), (anchor, row_start, col_start))
            owner_start = owner_index.astype(jnp.int32)
            held = lax.dynamic_slice(probe_sum, (owner_start, anchor, anchor, anchor), (1, 2, PATCH, PATCH))
            probe_sum = lax.dynamic_update_slice(probe_sum, held + probe_term[None], (owner_start, anchor, anchor, anchor))
            return (gradient, probe_sum)

        def passive(current_pair):
            return current_pair
        return (lax.cond(flat_rows[position] >= 0, active, passive, state_pair), None)
    start_pair = (jnp.zeros((2, NR, NC), jnp.float32), jnp.zeros((N_SCAN, 2, PATCH, PATCH), jnp.float32))
    final_pair, unused = lax.scan(visit, start_pair, jnp.arange(N_OBJ * per_band, dtype=jnp.int32))
    gradient, probe_sum = final_pair
    return (gradient, probe_sum / math.sqrt(N_OBJ * N_SCAN * CAP))
```

```python
import functools
import math

import jax
import jax.numpy as jnp
import ml_dtypes
import numpy as np
from jax import lax
from jax.experimental import pallas as pl
from jax.experimental.pallas import tpu as pltpu
from jax.sharding import PartitionSpec as P

MESH = pl.DeviceIdType.MESH
F32 = jnp.float32
BF16 = jnp.bfloat16

ORDER = [
    (0, 0), (1, 1), (3, 3), (1, 3), (3, 1), (0, 1), (1, 0), (0, 3),
    (3, 0), (2, 2), (1, 2), (2, 1), (3, 2), (2, 3), (0, 2), (2, 0),
]
CODES = [dz * 4 + dx for dz, dx in ORDER]
RP = 32
CH = 32
EC = 32


def dft_tables(length):
    grid = np.arange(length)
    angle = 2.0 * math.pi / length * (grid[:, None] * grid[None, :] % length)
    real = np.cos(angle) / math.sqrt(length)
    imag = -np.sin(angle) / math.sqrt(length)
    left = np.block([[real, -imag], [imag, real]])
    right = np.block([[real, imag], [-imag, real]])
    return left.astype(ml_dtypes.bfloat16), right.astype(ml_dtypes.bfloat16)


def code_of(n):
    return functools.reduce(lambda a, t: jnp.where(n == t, CODES[t], a), range(1, 16), jnp.int32(0))


def kernel(
    row_ref, col_ref, obj, probe, amps, ltab, rtab,
    out, pout,
    amp, ext, grad, term, patch, ebuf, hbuf, dbuf, bbuf, wide, pacc,
    strip_s, strip_r, low_s, low_r, corner_r,
    sib_s, sib_r, ysum, y_s, y_r, q_s, q_r, pg,
    rim_s, rim_r, lrim_s, lrim_r, crim_r,
    local_sem, halo_ss, halo_rs, amp_ss, amp_rs, sib_ss, sib_rs, y_ss, y_rs, q_ss, q_rs, g_ss, g_rs, rim_ss, rim_rs,
):
    me = lax.axis_index("scan")
    band = lax.axis_index("obj")
    z, x = me // 4, me % 4
    yy, core = band // 2, band % 2
    left, right = (me + 15) % 16, (me + 1) % 16
    above, below = (band + 7) % 8, (band + 1) % 8

    barrier = pltpu.get_barrier_semaphore()
    for d in range(1, 16):
        pl.semaphore_signal(barrier, inc=1, device_id={"scan": (me + d) % 16}, device_id_type=MESH)
    for d in range(1, 8):
        pl.semaphore_signal(barrier, inc=1, device_id={"obj": (band + d) % 8}, device_id_type=MESH)

    def remote(src, dst, ss, rs, where):
        return pltpu.make_async_remote_copy(
            src_ref=src, dst_ref=dst, send_sem=ss, recv_sem=rs, device_id=where, device_id_type=MESH
        )

    tile_in = []
    for p in range(2):
        for b in range(4):
            cp = pltpu.make_async_copy(
                obj.at[p, :, pl.ds(b * 128, 128)], ext.at[p, b, pl.ds(0, 512)], local_sem.at[p * 4 + b]
            )
            cp.start()
            tile_in.append(cp)
    own_in = []
    for s in range(2):
        cp = pltpu.make_async_copy(amps.at[2 * me + s], amp.at[s * 16], local_sem.at[8 + s])
        cp.start()
        own_in.append(cp)
    for cp in tile_in:
        cp.wait()

    def round_rows(i, c):
        rows = pl.ds(pl.multiple_of(i * 64, 64), 64)
        for p in range(2):
            for b in range(4):
                v = ext[p, b, rows, :].astype(BF16)
                ext[p, b, rows, :] = v.astype(F32)
                if b < 2:
                    strip_s[p, b, rows, :] = v
        return c

    lax.fori_loop(0, 8, round_rows, 0)

    def low_rows(i, c):
        rows = pl.ds(pl.multiple_of(i * 64, 64), 64)
        for p in range(2):
            for b in range(4):
                low_s[p, b, rows, :] = ext[p, b, rows, :].astype(BF16)
        return c

    lax.fori_loop(0, 4, low_rows, 0)

    pl.semaphore_wait(barrier, 22)

    strip_cp = remote(strip_s, strip_r, halo_ss.at[0], halo_rs.at[0], {"scan": left})
    strip_cp.start()
    low_cp = remote(low_s, low_r, halo_ss.at[1], halo_rs.at[1], {"obj": above})
    low_cp.start()

    def amp_copy(t, s):
        dz, dx = ORDER[t]
        target = ((z + dz) % 4) * 4 + (x + dx) % 4
        at = s * 16 + CODES[t]
        return remote(amps.at[2 * target + s], amp.at[at], amp_ss.at[at], amp_rs.at[at], {"scan": target})

    for s in range(2):
        for t in range(1, 16):
            amp_copy(t, s).start()

    def zero_rows(i, c):
        rows = pl.ds(pl.multiple_of(i * 64, 64), 64)
        nil = jnp.zeros((64, 128), F32)
        for p in range(2):
            for b in range(3):
                ext[p, 6 + b, rows, :] = nil
            for b in range(6):
                grad[p, b, rows, :] = nil
        return c

    lax.fori_loop(0, 12, zero_rows, 0)

    def zero_terms(i, c):
        nil = jnp.zeros((RP, 128), F32)
        term[i, 0:RP, :] = nil
        term[i, RP + 256 : RP + 256 + RP, :] = nil
        return c

    lax.fori_loop(0, 24, zero_terms, 0)
    term[24] = jnp.zeros((256 + 2 * RP, 128), F32)

    strip_cp.wait_recv()
    corner_cp = remote(
        strip_r.at[:, :, pl.ds(0, 256)], corner_r, halo_ss.at[2], halo_rs.at[2], {"obj": above}
    )
    corner_cp.start()

    def strip_rows(i, c):
        rows = pl.ds(pl.multiple_of(i * 64, 64), 64)
        for p in range(2):
            for b in range(2):
                ext[p, 4 + b, rows, :] = strip_r[p, b, rows, :].astype(F32)
        return c

    lax.fori_loop(0, 8, strip_rows, 0)
    low_cp.wait_recv()

    def low_in(i, c):
        rows = pl.ds(pl.multiple_of(i * 64, 64), 64)
        dest = pl.ds(pl.multiple_of(512 + i * 64, 64), 64)
        for p in range(2):
            for b in range(4):
                ext[p, b, dest, :] = low_r[p, b, rows, :].astype(F32)
        return c

    lax.fori_loop(0, 4, low_in, 0)
    corner_cp.wait_recv()

    def corner_in(i, c):
        rows = pl.ds(pl.multiple_of(i * 64, 64), 64)
        dest = pl.ds(pl.multiple_of(512 + i * 64, 64), 64)
        for p in range(2):
            for b in range(2):
                ext[p, 4 + b, dest, :] = corner_r[p, b, rows, :].astype(F32)
        return c

    lax.fori_loop(0, 4, corner_in, 0)
    for cp in own_in:
        cp.wait()

    lane = lax.broadcasted_iota(jnp.int32, (EC, 128), 1)

    def owner_of(n):
        code = code_of(n)
        dz, dx = code // 4, code % 4
        return code, ((z + 4 - dz) % 4) * 4 + (x + 4 - dx) % 4

    def pair(s, i, u):
        slots = []
        for a in range(2):
            code, owner = owner_of(2 * i + a)
            at = s * 16 + code
            if a == 0:

                @pl.when(i > 0)
                def _():
                    pltpu.make_async_remote_copy(
                        src_ref=amp.at[at], dst_ref=amp.at[at], send_sem=amp_ss.at[at], recv_sem=amp_rs.at[at],
                        device_id={"scan": right}, device_id_type=MESH,
                    ).wait_recv()
            else:
                pltpu.make_async_remote_copy(
                    src_ref=amp.at[at], dst_ref=amp.at[at], send_sem=amp_ss.at[at], recv_sem=amp_rs.at[at],
                    device_id={"scan": right}, device_id_type=MESH,
                ).wait_recv()
            row = row_ref[owner * 2 + s]
            col = col_ref[owner * 2 + s]
            live = row >= 0
            r0 = jnp.maximum(row, 0)
            c0 = jnp.maximum(col, 0)
            block = jnp.where(live, c0 // 128, 6)
            slots.append((at, r0, block, c0 % 128))
        for a, (at, r0, block, shift) in enumerate(slots):
            for rc in range(0, 256, EC):
                f = []
                for p in range(2):
                    raw = [
                        pltpu.roll(ext[p, block + q, pl.ds(r0 + rc, EC), :], (128 - shift) % 128, 1) for q in range(3)
                    ]
                    f.append([jnp.where(lane < 128 - shift, raw[b], raw[b + 1]) for b in range(2)])
                for b in range(2):
                    lanes = slice(b * 128, b * 128 + 128)
                    fr, fi = f[0][b], f[1][b]
                    pr, pi = probe[0, rc : rc + EC, lanes], probe[1, rc : rc + EC, lanes]
                    patch[a, 0, rc : rc + EC, lanes] = fr.astype(BF16)
                    patch[a, 1, rc : rc + EC, lanes] = fi.astype(BF16)
                    here = slice(a * 256 + b * 128, a * 256 + b * 128 + 128)
                    ebuf[rc : rc + EC, here] = (pr * fr - pi * fi).astype(BF16)
                    ebuf[256 + rc : 256 + rc + EC, here] = (pr * fi + pi * fr).astype(BF16)
        half = jnp.dot(ltab[...], ebuf[...], preferred_element_type=F32).astype(BF16)
        for a in range(2):
            for p in range(2):
                hbuf[a * 256 : a * 256 + 256, p * 256 : p * 256 + 256] = half[
                    p * 256 : p * 256 + 256, a * 256 : a * 256 + 256
                ]
        wide[...] = jnp.dot(hbuf[...], rtab[...], preferred_element_type=F32)
        for a, (at, r0, block, shift) in enumerate(slots):
            for rc in range(0, 256, EC):
                fr = wide[a * 256 + rc : a * 256 + rc + EC, 0:256]
                fi = wide[a * 256 + rc : a * 256 + rc + EC, 256:512]
                m = amp[at, rc : rc + EC, :].astype(F32)
                scale = m * lax.rsqrt(jnp.maximum(fr * fr + fi * fi, 0.01)) - 1.0
                dbuf[rc : rc + EC, a * 256 : a * 256 + 256] = (fr * scale).astype(BF16)
                dbuf[256 + rc : 256 + rc + EC, a * 256 : a * 256 + 256] = (fi * scale).astype(BF16)
        back = jnp.dot(rtab[...], dbuf[...], preferred_element_type=F32).astype(BF16)
        for a in range(2):
            for p in range(2):
                bbuf[a * 256 : a * 256 + 256, p * 256 : p * 256 + 256] = back[
                    p * 256 : p * 256 + 256, a * 256 : a * 256 + 256
                ]
        wide[...] = jnp.dot(bbuf[...], ltab[...], preferred_element_type=F32)
        for a, (at, r0, block, shift) in enumerate(slots):
            base = (u * 2 + a) * 6
            n = 2 * i + a
            for rc in range(0, 256, EC):
                rows = slice(rc, rc + EC)
                trail = [None, None]
                for b in range(2):
                    lanes = slice(b * 128, b * 128 + 128)
                    nr = wide[a * 256 + rc : a * 256 + rc + EC, b * 128 : b * 128 + 128]
                    ni = wide[a * 256 + rc : a * 256 + rc + EC, 256 + b * 128 : 256 + b * 128 + 128]
                    pr, pi = probe[0, rows, lanes], probe[1, rows, lanes]
                    fr, fi = patch[a, 0, rows, lanes].astype(F32), patch[a, 1, rows, lanes].astype(F32)
                    tt = (pr * nr + pi * ni, pr * ni - pi * nr)
                    for p in range(2):
                        turned = pltpu.roll(tt[p], shift, 1)
                        before = trail[p] if b else jnp.zeros_like(turned)
                        term[base + p * 3 + b, RP + rc : RP + rc + EC, :] = jnp.where(lane >= shift, turned, before)
                        trail[p] = turned
                    pacc[n, 0, rows, lanes] = jnp.where(s == 0, 0.0, pacc[n, 0, rows, lanes]) + (fr * nr + fi * ni)
                    pacc[n, 1, rows, lanes] = jnp.where(s == 0, 0.0, pacc[n, 1, rows, lanes]) + (fr * ni - fi * nr)
                for p in range(2):
                    term[base + p * 3 + 2, RP + rc : RP + rc + EC, :] = jnp.where(
                        lane >= shift, jnp.zeros_like(trail[p]), trail[p]
                    )

    def gather(s, v):
        places = []
        for w in range(4):
            code, owner = owner_of(4 * v + w)
            row = jnp.maximum(row_ref[owner * 2 + s], 0)
            block = jnp.maximum(col_ref[owner * 2 + s], 0) // 128
            places.append((row, block))
        picks = [
            [
                [
                    jnp.where((b - block >= 0) & (b - block < 3), (w * 2 + p) * 3 + b - block, 24)
                    for w, (row, block) in enumerate(places)
                ]
                for b in range(6)
            ]
            for p in range(2)
        ]

        def rows_of(ic, c):
            rows = pl.ds(pl.multiple_of(ic * CH, CH), CH)
            starts = [jnp.clip(ic * CH - row, -RP, 256) + RP for row, block in places]
            for b in range(6):
                for p in range(2):
                    acc = grad[p, b, rows, :]
                    for w in range(4):
                        acc = acc + term[picks[p][b][w], pl.ds(starts[w], CH), :]
                    grad[p, b, rows, :] = acc
            return c

        lax.fori_loop(0, 768 // CH, rows_of, 0)

    def sib_copy(i):
        return remote(sib_s.at[i], sib_r.at[i], sib_ss.at[i], sib_rs.at[i], {"obj": 2 * yy + 1 - core})

    def y_copy(i, d):
        to = (yy + d) % 4
        return remote(
            y_s.at[i, to], y_r.at[i, d - 1], y_ss.at[i * 3 + d - 1], y_rs.at[i * 3 + d - 1], {"obj": 2 * to + core}
        )

    def q_copy(i, a):
        code, owner = owner_of(2 * i + a)
        return remote(q_s.at[i, a], q_r.at[code], q_ss.at[code], q_rs.at[code], {"scan": owner})

    mine = pl.ds(pl.multiple_of(core * 128, 128), 128)
    other = pl.ds(pl.multiple_of((1 - core) * 128, 128), 128)

    def sib_stage(i):
        for a in range(2):
            for p in range(2):
                sib_s[i, a, p] = pacc[2 * i + a, p, other, :].astype(BF16)
        sib_copy(i).start()

    def y_stage(i):
        sib_copy(i).wait_recv()
        for a in range(2):
            for p in range(2):
                total = pacc[2 * i + a, p, mine, :] + sib_r[i, a, p].astype(F32)
                for q in range(4):
                    ysum[i, q, a, p] = total[q * 32 : q * 32 + 32]
                    y_s[i, q, a, p] = total[q * 32 : q * 32 + 32].astype(BF16)
        for d in range(1, 4):
            y_copy(i, d).start()

    def q_stage(i):
        for d in range(1, 4):
            y_copy(i, d).wait_recv()
        for a in range(2):
            for p in range(2):
                total = ysum[i, yy, a, p]
                for d in range(3):
                    total = total + y_r[i, d, a, p].astype(F32)
                q_s[i, a, p] = total.astype(BF16)

        @pl.when(i > 0)
        def _():
            q_copy(i, 0).start()

        q_copy(i, 1).start()

    def double_step(v2, c):
        s, v = v2 // 4, v2 % 4

        def single(u, c):
            i = 2 * v + u

            @pl.when((s == 1) & (i >= 1))
            def _():
                y_stage(i - 1)

            @pl.when((s == 1) & (i >= 2))
            def _():
                q_stage(i - 2)

            pair(s, i, u)

            @pl.when(s == 1)
            def _():
                sib_stage(i)

            return c

        lax.fori_loop(0, 2, single, 0)
        gather(s, v)
        return c

    lax.fori_loop(0, 8, double_step, 0)

    def corner_out(i, c):
        rows = pl.ds(pl.multiple_of(i * 64, 64), 64)
        low = pl.ds(pl.multiple_of(512 + i * 64, 64), 64)
        for p in range(2):
            for b in range(6):
                lrim_s[(b + 2) % 6 // 2, p, b % 2, rows, :] = grad[p, b, low, :].astype(BF16)
        return c

    lax.fori_loop(0, 4, corner_out, 0)
    crim_cp = remote(lrim_s.at[0], crim_r, rim_ss.at[0], rim_rs.at[0], {"obj": below})
    crim_cp.start()

    def rim_low_half(i, c):
        rows = pl.ds(pl.multiple_of(i * 64, 64), 64)
        src = pl.ds(pl.multiple_of(256 + i * 64, 64), 64)
        for p in range(2):
            for b in range(2):
                rim_s[1, p, b, rows, :] = grad[p, 4 + b, src, :].astype(BF16)
        return c

    lax.fori_loop(0, 4, rim_low_half, 0)
    rim_b = remote(rim_s.at[1], rim_r.at[1], rim_ss.at[1], rim_rs.at[1], {"scan": right})
    rim_b.start()
    lrim_cp = remote(lrim_s.at[pl.ds(1, 2)], lrim_r, rim_ss.at[2], rim_rs.at[2], {"obj": below})
    lrim_cp.start()
    y_stage(7)
    q_stage(6)
    crim_cp.wait_recv()

    def rim_top_half(i, c):
        rows = pl.ds(pl.multiple_of(i * 64, 64), 64)
        for p in range(2):
            for b in range(2):
                rim_s[0, p, b, rows, :] = (grad[p, 4 + b, rows, :] + crim_r[p, b, rows, :].astype(F32)).astype(BF16)
        return c

    lax.fori_loop(0, 4, rim_top_half, 0)
    rim_t = remote(rim_s.at[0], rim_r.at[0], rim_ss.at[3], rim_rs.at[3], {"scan": right})
    rim_t.start()
    q_stage(7)

    def out_copy(p, b, h):
        rows = pl.ds(h * 256, 256)
        return pltpu.make_async_copy(
            grad.at[p, b, rows], out.at[p, rows, pl.ds(b * 128, 128)], local_sem.at[(p * 4 + b) * 2 + h]
        )

    for p in range(2):
        for b in range(2, 4):
            out_copy(p, b, 1).start()

    for n in range(1, 16):
        code = CODES[n]
        remote(q_s.at[0, 0], q_r.at[code], q_ss.at[code], q_rs.at[code], {"scan": right}).wait_recv()
    piece = core * 4 + yy
    prow = pl.ds(pl.multiple_of(piece * 32, 32), 32)
    for p in range(2):
        total = q_s[0, 0, p].astype(F32)
        for n in range(1, 16):
            total = total + q_r[CODES[n], p].astype(F32)
        pg[p, prow, :] = total * (1.0 / 16.0)

    def g_copy(d):
        to = (band + d) % 8
        return remote(pg.at[:, prow], pg.at[:, prow], g_ss.at[d - 1], g_rs.at[d - 1], {"obj": to})

    for d in range(1, 8):
        g_copy(d).start()

    lrim_cp.wait_recv()

    def add_low(i, c):
        rows = pl.ds(pl.multiple_of(i * 64, 64), 64)
        for p in range(2):
            for b in range(4):
                grad[p, b, rows, :] = grad[p, b, rows, :] + lrim_r[b // 2, p, b % 2, rows, :].astype(F32)
        return c

    lax.fori_loop(0, 4, add_low, 0)
    for p in range(2):
        for b in range(2, 4):
            out_copy(p, b, 0).start()
    for h, cp in ((1, rim_b), (0, rim_t)):
        cp.wait_recv()

        def add_rim(i, c):
            rows = pl.ds(pl.multiple_of(i * 64, 64), 64)
            dest = pl.ds(pl.multiple_of(h * 256 + i * 64, 64), 64)
            for p in range(2):
                for b in range(2):
                    grad[p, b, dest, :] = grad[p, b, dest, :] + rim_r[h, p, b, rows, :].astype(F32)
            return c

        lax.fori_loop(0, 4, add_rim, 0)
        for p in range(2):
            for b in range(2):
                out_copy(p, b, h).start()

    for d in range(1, 8):
        frm = (band + 8 - d) % 8
        frow = pl.ds(pl.multiple_of(((frm % 2) * 4 + frm // 2) * 32, 32), 32)
        remote(pg.at[:, frow], pg.at[:, frow], g_ss.at[d - 1], g_rs.at[d - 1], {"obj": frm}).wait_recv()
    pcp = pltpu.make_async_copy(pg, pout, local_sem.at[16])
    pcp.start()

    for cp in (strip_cp, low_cp, corner_cp, crim_cp, rim_b, lrim_cp, rim_t):
        cp.wait_send()
    for s in range(2):
        for t in range(1, 16):
            amp_copy(t, s).wait_send()

    def drain(i, c):
        sib_copy(i).wait_send()
        for d in range(1, 4):
            y_copy(i, d).wait_send()

        @pl.when(i > 0)
        def _():
            q_copy(i, 0).wait_send()

        q_copy(i, 1).wait_send()
        return c

    lax.fori_loop(0, 8, drain, 0)
    for d in range(1, 8):
        g_copy(d).wait_send()
    for p in range(2):
        for b in range(4):
            for h in range(2):
                out_copy(p, b, h).wait()
    pcp.wait()


def on_device(object_field, probe, amplitudes, corner_row, corner_col):
    ltab, rtab = dft_tables(256)
    vm = pltpu.VMEM
    dma = pltpu.SemaphoreType.DMA
    anywhere = pl.BlockSpec(memory_space=pl.ANY)
    inside = pl.BlockSpec(memory_space=pltpu.VMEM)
    scalar = pl.BlockSpec(memory_space=pltpu.SMEM)
    object_grad, probe_grad = pl.pallas_call(
        kernel,
        out_shape=(
            jax.ShapeDtypeStruct((2, 512, 512), F32),
            jax.ShapeDtypeStruct((2, 256, 256), F32),
        ),
        in_specs=[scalar, scalar, anywhere, inside, anywhere, inside, inside],
        out_specs=(anywhere, anywhere),
        scratch_shapes=[
            vm((32, 256, 256), BF16),
            vm((2, 9, 768, 128), F32),
            vm((2, 6, 768, 128), F32),
            vm((25, 256 + 2 * RP, 128), F32),
            vm((2, 2, 256, 256), BF16),
            vm((512, 512), BF16),
            vm((512, 512), BF16),
            vm((512, 512), BF16),
            vm((512, 512), BF16),
            vm((512, 512), F32),
            vm((16, 2, 256, 256), F32),
            vm((2, 2, 512, 128), BF16),
            vm((2, 2, 512, 128), BF16),
            vm((2, 4, 256, 128), BF16),
            vm((2, 4, 256, 128), BF16),
            vm((2, 2, 256, 128), BF16),
            vm((8, 2, 2, 128, 256), BF16),
            vm((8, 2, 2, 128, 256), BF16),
            vm((8, 4, 2, 2, 32, 256), F32),
            vm((8, 4, 2, 2, 32, 256), BF16),
            vm((8, 3, 2, 2, 32, 256), BF16),
            vm((8, 2, 2, 32, 256), BF16),
            vm((16, 2, 32, 256), BF16),
            vm((2, 256, 256), F32),
            vm((2, 2, 2, 256, 128), BF16),
            vm((2, 2, 2, 256, 128), BF16),
            vm((3, 2, 2, 256, 128), BF16),
            vm((2, 2, 2, 256, 128), BF16),
            vm((2, 2, 256, 128), BF16),
            dma((17,)),
            dma((3,)), dma((3,)),
            dma((32,)), dma((32,)),
            dma((8,)), dma((8,)),
            dma((24,)), dma((24,)),
            dma((16,)), dma((16,)),
            dma((7,)), dma((7,)),
            dma((4,)), dma((4,)),
        ],
        compiler_params=pltpu.CompilerParams(
            collective_id=0, has_side_effects=True, vmem_limit_bytes=62 * 2**20
        ),
        cost_estimate=pl.CostEstimate(flops=32 * 16 * 2 * 256**3, bytes_accessed=10 * 2**20, transcendentals=32 * 65536),
    )(
        corner_row.reshape(32), corner_col.reshape(32), object_field, probe, amplitudes[0],
        jnp.asarray(ltab), jnp.asarray(rtab),
    )
    return object_grad, probe_grad[None]


def solution(mesh):
    return jax.shard_map(
        on_device,
        mesh=mesh,
        in_specs=(
            P(None, "obj", "scan"),
            P(),
            P("obj", "scan", None, None),
            P("obj", "scan", None),
            P("obj", "scan", None),
        ),
        out_specs=(P(None, "obj", "scan"), P("scan", None, None, None)),
        check_vma=False,
    )
```

```python
import functools
import math

import jax
import jax.numpy as jnp
import ml_dtypes
import numpy as np
from jax import lax
from jax.experimental import pallas as pl
from jax.experimental.pallas import tpu as pltpu
from jax.sharding import PartitionSpec as P

MESH = pl.DeviceIdType.MESH
F32 = jnp.float32
BF16 = jnp.bfloat16

ORDER = [
    (0, 0), (1, 1), (3, 1), (1, 0), (3, 0), (0, 1), (2, 1), (1, 3),
    (3, 3), (1, 2), (3, 2), (0, 3), (2, 3), (2, 2), (0, 2), (2, 0),
]
CODES = [dz * 4 + dx for dz, dx in ORDER]
GROUPS = [(1, 4), (4, 8), (8, 12), (12, 14), (14, 16)]
RP = 32
CH = 32
EC = 32
PLAN = [
    ("X", 0), ("H", 0), ("X", 1), ("F", 0), ("H", 1), ("X", 2), ("F", 1), ("H", 2), ("X", 3), ("F", 2),
    ("H", 3), ("F", 3), ("A", 0), ("A", 1), ("A", 2), ("A", 3), ("D", 0), ("B", 0), ("D", 1), ("B", 1),
    ("D", 2), ("N", 0), ("B", 2), ("D", 3), ("N", 1), ("T", 0), ("B", 3), ("T", 1), ("N", 2), ("T", 2),
    ("N", 3), ("T", 3),
]


def dft_tables(length):
    grid = np.arange(length)
    angle = 2.0 * math.pi / length * (grid[:, None] * grid[None, :] % length)
    real = np.cos(angle) / math.sqrt(length)
    imag = -np.sin(angle) / math.sqrt(length)
    left = np.block([[real, -imag], [imag, real]])
    right = np.block([[real, imag], [-imag, real]])
    return left.astype(ml_dtypes.bfloat16), right.astype(ml_dtypes.bfloat16)


def code_of(n):
    return functools.reduce(lambda a, t: jnp.where(n == t, CODES[t], a), range(1, 16), jnp.int32(0))


def kernel(
    row_ref, col_ref, obj, probe, amps, ltab, rtab,
    out, rim_r, lrim_r, g_r,
    amp, ext, grad, term, patch, ebuf, hbuf, dbuf, bbuf, wide, pacc,
    strip_s, strip_r, low_s, low_r, corner_r,
    sib_s, sib_r, kept, y_s, y_r, q_s, q_r, x_s, x_r, g_s,
    rim_s, lrim_s, crim_r,
    local_sem, halo_ss, halo_rs, amp_ss, amp_rs, sib_ss, sib_rs, y_ss, y_rs, q_ss, q_rs, x_ss, x_rs, g_ss, g_rs, rim_ss, rim_rs,
):
    me = lax.axis_index("scan")
    band = lax.axis_index("obj")
    z, x = me // 4, me % 4
    yy, core = band // 2, band % 2
    left, right = (me + 15) % 16, (me + 1) % 16
    above, below = (band + 7) % 8, (band + 1) % 8

    barrier = pltpu.get_barrier_semaphore()
    for d in range(1, 16):
        pl.semaphore_signal(barrier, inc=1, device_id={"scan": (me + d) % 16}, device_id_type=MESH)
    for d in range(1, 8):
        pl.semaphore_signal(barrier, inc=1, device_id={"obj": (band + d) % 8}, device_id_type=MESH)

    def remote(src, dst, ss, rs, where):
        return pltpu.make_async_remote_copy(
            src_ref=src, dst_ref=dst, send_sem=ss, recv_sem=rs, device_id=where, device_id_type=MESH
        )

    tile_in = []
    for p in range(2):
        for b in range(4):
            cp = pltpu.make_async_copy(
                obj.at[p, :, pl.ds(b * 128, 128)], ext.at[p, b, pl.ds(0, 512)], local_sem.at[p * 4 + b]
            )
            cp.start()
            tile_in.append(cp)
    own_in = []
    for s in range(2):
        cp = pltpu.make_async_copy(amps.at[2 * me + s], amp.at[s * 16], local_sem.at[8 + s])
        cp.start()
        own_in.append(cp)
    pl.semaphore_wait(barrier, 22)

    def amp_copy(t, s):
        dz, dx = ORDER[t]
        target = ((z + dz) % 4) * 4 + (x + dx) % 4
        at = s * 16 + CODES[t]
        return remote(amps.at[2 * target + s], amp.at[at], amp_ss.at[at], amp_rs.at[at], {"scan": target})

    sends = [(t, s) for g, e in GROUPS for s in range(2) for t in range(g, e)]
    for t, s in sends[:6]:
        amp_copy(t, s).start()
    for cp in tile_in:
        cp.wait()

    def round_rows(i, c):
        rows = pl.ds(pl.multiple_of(i * 64, 64), 64)
        for p in range(2):
            for b in range(4):
                v = ext[p, b, rows, :].astype(BF16)
                ext[p, b, rows, :] = v.astype(F32)
                if b < 2:
                    strip_s[i // 4, p, b, pl.ds(pl.multiple_of(i % 4 * 64, 64), 64), :] = v
        return c

    lax.fori_loop(0, 8, round_rows, 0)

    def low_rows(i, c):
        rows = pl.ds(pl.multiple_of(i * 64, 64), 64)
        for p in range(2):
            for b in range(4):
                low_s[p, b, rows, :] = ext[p, b, rows, :].astype(BF16)
        return c

    lax.fori_loop(0, 4, low_rows, 0)

    strip_cps = [
        remote(strip_s.at[h], strip_r.at[h], halo_ss.at[3 * h], halo_rs.at[3 * h], {"scan": left}) for h in range(2)
    ]
    for cp in strip_cps:
        cp.start()
    low_cp = remote(low_s, low_r, halo_ss.at[1], halo_rs.at[1], {"obj": above})
    low_cp.start()

    for t, s in sends[6:]:
        amp_copy(t, s).start()

    def zero_rows(i, c):
        rows = pl.ds(pl.multiple_of(i * 64, 64), 64)
        nil = jnp.zeros((64, 128), F32)
        for p in range(2):
            for b in range(3):
                ext[p, 6 + b, rows, :] = nil
            for b in range(6):
                grad[p, b, rows, :] = nil
        return c

    lax.fori_loop(0, 12, zero_rows, 0)

    def zero_terms(i, c):
        nil = jnp.zeros((RP, 128), F32)
        term[i, 0:RP, :] = nil
        term[i, RP + 256 : RP + 256 + RP, :] = nil
        return c

    lax.fori_loop(0, 24, zero_terms, 0)
    term[24] = jnp.zeros((256 + 2 * RP, 128), F32)

    strip_cps[0].wait_recv()
    corner_cp = remote(strip_r.at[0], corner_r, halo_ss.at[2], halo_rs.at[2], {"obj": above})
    corner_cp.start()

    def strip_rows(h):
        def rows_of(i, c):
            rows = pl.ds(pl.multiple_of(i * 64, 64), 64)
            dest = pl.ds(pl.multiple_of(h * 256 + i * 64, 64), 64)
            for p in range(2):
                for b in range(2):
                    ext[p, 4 + b, dest, :] = strip_r[h, p, b, rows, :].astype(F32)
            return c

        lax.fori_loop(0, 4, rows_of, 0)

    strip_rows(0)
    low_cp.wait_recv()

    def low_in(i, c):
        rows = pl.ds(pl.multiple_of(i * 64, 64), 64)
        dest = pl.ds(pl.multiple_of(512 + i * 64, 64), 64)
        for p in range(2):
            for b in range(4):
                ext[p, b, dest, :] = low_r[p, b, rows, :].astype(F32)
        return c

    lax.fori_loop(0, 4, low_in, 0)
    strip_cps[1].wait_recv()
    strip_rows(1)
    corner_cp.wait_recv()

    def corner_in(i, c):
        rows = pl.ds(pl.multiple_of(i * 64, 64), 64)
        dest = pl.ds(pl.multiple_of(512 + i * 64, 64), 64)
        for p in range(2):
            for b in range(2):
                ext[p, 4 + b, dest, :] = corner_r[p, b, rows, :].astype(F32)
        return c

    lax.fori_loop(0, 4, corner_in, 0)
    for cp in own_in:
        cp.wait()

    lane = lax.broadcasted_iota(jnp.int32, (EC, 128), 1)

    def owner_of(n):
        code = code_of(n)
        dz, dx = code // 4, code % 4
        return code, ((z + 4 - dz) % 4) * 4 + (x + 4 - dx) % 4

    def amp_wait(at):
        pltpu.make_async_remote_copy(
            src_ref=amp.at[at], dst_ref=amp.at[at], send_sem=amp_ss.at[at], recv_sem=amp_rs.at[at],
            device_id={"scan": right}, device_id_type=MESH,
        ).wait_recv()

    def four(v):
        slots = []
        for a in range(2):
            code, owner = owner_of(2 * v + a)
            for s in range(2):
                at = s * 16 + code
                row = row_ref[s, owner]
                col = col_ref[s, owner]
                c0 = jnp.maximum(col, 0)
                slots.append((at, jnp.maximum(row, 0), jnp.where(row >= 0, c0 // 128, 6), c0 % 128))

        def arrived(k):
            if k < 2:
                pl.when(v > 0)(functools.partial(amp_wait, slots[k][0]))
            else:
                amp_wait(slots[k][0])

        def exit_wave(k):
            at, r0, block, shift = slots[k]
            for rc in range(0, 256, EC):
                rows = slice(rc, rc + EC)
                f = []
                for p in range(2):
                    raw = [ext[p, block + q, pl.ds(r0 + rc, EC), :] for q in range(3)]
                    f.append([
                        pltpu.roll(jnp.where(lane >= shift, raw[b], raw[b + 1]).astype(BF16), (128 - shift) % 128, 1)
                        for b in range(2)
                    ])
                for b in range(2):
                    lanes = slice(b * 128, b * 128 + 128)
                    fr, fi = f[0][b].astype(F32), f[1][b].astype(F32)
                    pr, pi = probe[0, rows, lanes], probe[1, rows, lanes]
                    patch[k, 0, rows, lanes] = f[0][b]
                    patch[k, 1, rows, lanes] = f[1][b]
                    ebuf[k, rows, lanes] = (pr * fr - pi * fi).astype(BF16)
                    ebuf[k, 256 + rc : 256 + rc + EC, lanes] = (pr * fi + pi * fr).astype(BF16)

        def half_to(k):
            h = jnp.dot(ltab[...], ebuf[k], preferred_element_type=F32).astype(BF16)
            hbuf[k, :, 0:256] = h[0:256]
            hbuf[k, :, 256:512] = h[256:512]

        def far_to(k):
            wide[k] = jnp.dot(hbuf[k], rtab[...], preferred_element_type=F32)

        def differ(k):
            at = slots[k][0]
            for rc in range(0, 256, EC):
                rows = slice(rc, rc + EC)
                fr, fi = wide[k, rows, 0:256], wide[k, rows, 256:512]
                m = amp[at, rows, :].astype(F32)
                scale = m * lax.rsqrt(jnp.maximum(fr * fr + fi * fi, 0.01)) - 1.0
                dbuf[k, rows, :] = (fr * scale).astype(BF16)
                dbuf[k, 256 + rc : 256 + rc + EC, :] = (fi * scale).astype(BF16)

        def back_to(k):
            h = jnp.dot(rtab[...], dbuf[k], preferred_element_type=F32).astype(BF16)
            bbuf[k, :, 0:256] = h[0:256]
            bbuf[k, :, 256:512] = h[256:512]

        def near_to(k):
            wide[4 + k] = jnp.dot(bbuf[k], ltab[...], preferred_element_type=F32)

        def terms(k):
            at, r0, block, shift = slots[k]
            n, second = k // 2, k % 2 == 1
            for rc in range(0, 256, EC):
                rows = slice(rc, rc + EC)
                trail = [None, None]
                for b in range(2):
                    lanes = slice(b * 128, b * 128 + 128)
                    nr = wide[4 + k, rows, b * 128 : b * 128 + 128]
                    ni = wide[4 + k, rows, 256 + b * 128 : 256 + b * 128 + 128]
                    pr, pi = probe[0, rows, lanes], probe[1, rows, lanes]
                    fr, fi = patch[k, 0, rows, lanes].astype(F32), patch[k, 1, rows, lanes].astype(F32)
                    tt = (pr * nr + pi * ni, pr * ni - pi * nr)
                    for p in range(2):
                        turned = pltpu.roll(tt[p].astype(BF16), shift, 1).astype(F32)
                        before = trail[p] if b else jnp.zeros_like(turned)
                        term[k * 6 + p * 3 + b, RP + rc : RP + rc + EC, :] = jnp.where(lane >= shift, turned, before)
                        trail[p] = turned
                    pt = (fr * nr + fi * ni, fr * ni - fi * nr)
                    for p in range(2):
                        pacc[n, p, rows, lanes] = pacc[n, p, rows, lanes] + pt[p] if second else pt[p]
                for p in range(2):
                    term[k * 6 + p * 3 + 2, RP + rc : RP + rc + EC, :] = jnp.where(
                        lane >= shift, jnp.zeros_like(trail[p]), trail[p]
                    )

        stages = {"A": arrived, "X": exit_wave, "H": half_to, "F": far_to, "D": differ, "B": back_to, "N": near_to, "T": terms}
        for stage, k in PLAN:
            stages[stage](k)

    def gather(v, blocks):
        places = []
        for w in range(4):
            code, owner = owner_of(2 * v + w // 2)
            row = jnp.maximum(row_ref[w % 2, owner], 0)
            block = jnp.maximum(col_ref[w % 2, owner], 0) // 128
            places.append((row, block))
        picks = [
            [
                [
                    jnp.where((b - block >= 0) & (b - block < 3), w * 6 + p * 3 + b - block, 24)
                    for w, (row, block) in enumerate(places)
                ]
                for b in range(6)
            ]
            for p in range(2)
        ]

        def rows_of(ic, c):
            rows = pl.ds(pl.multiple_of(ic * CH, CH), CH)
            starts = [jnp.clip(ic * CH - row, -RP, 256) + RP for row, block in places]
            for b in blocks:
                for p in range(2):
                    acc = grad[p, b, rows, :]
                    for w in range(4):
                        acc = acc + term[picks[p][b][w], pl.ds(starts[w], CH), :]
                    grad[p, b, rows, :] = acc
            return c

        lax.fori_loop(0, 768 // CH, rows_of, 0)

    def sib_copy(i):
        return remote(sib_s.at[i], sib_r.at[i], sib_ss.at[i], sib_rs.at[i], {"obj": 2 * yy + 1 - core})

    def y_copy(i, d):
        to = (yy + d) % 4
        return remote(
            y_s.at[i, to], y_r.at[i, d - 1], y_ss.at[i * 3 + d - 1], y_rs.at[i * 3 + d - 1], {"obj": 2 * to + core}
        )

    def q_copy(i, a):
        code, owner = owner_of(2 * i + a)
        return remote(q_s.at[i, a], q_r.at[code], q_ss.at[code], q_rs.at[code], {"scan": owner // 4 * 4 + x})

    mine = pl.ds(pl.multiple_of(core * 128, 128), 128)
    other = pl.ds(pl.multiple_of((1 - core) * 128, 128), 128)

    def sib_stage(i):
        for a in range(2):
            for p in range(2):
                sib_s[i, a, p] = pacc[a, p, other, :].astype(BF16)
                kept[i % 2, a, p] = pacc[a, p, mine, :]
        sib_copy(i).start()

    def y_stage(i):
        sib_copy(i).wait_recv()
        for a in range(2):
            for p in range(2):
                total = kept[i % 2, a, p] + sib_r[i, a, p].astype(F32)
                for q in range(4):
                    y_s[i, q, a, p] = total[q * 32 : q * 32 + 32].astype(BF16)
        for d in range(1, 4):
            y_copy(i, d).start()

    def q_stage(i):
        for d in range(1, 4):
            y_copy(i, d).wait_recv()
        for a in range(2):
            for p in range(2):
                total = y_s[i, yy, a, p].astype(F32)
                for d in range(3):
                    total = total + y_r[i, d, a, p].astype(F32)
                q_s[i, a, p] = total.astype(BF16)

        for a in range(2):
            code, owner = owner_of(2 * i + a)

            @pl.when(code >= 4)
            def _():
                q_copy(i, a).start()

            @pl.when(code < 4)
            def _():
                q_r[code] = q_s[i, a]

    def step(v, c):
        @pl.when(v >= 1)
        def _():
            y_stage(v - 1)

        @pl.when(v >= 2)
        def _():
            q_stage(v - 2)

        four(v)
        sib_stage(v)
        gather(v, (4, 5))

        @pl.when(v < 7)
        def _():
            gather(v, (0, 1, 2, 3))

        return c

    lax.fori_loop(0, 8, step, 0)

    def rim_low_half(i, c):
        rows = pl.ds(pl.multiple_of(i * 64, 64), 64)
        src = pl.ds(pl.multiple_of(256 + i * 64, 64), 64)
        for p in range(2):
            for b in range(2):
                rim_s[1, p, b, rows, :] = grad[p, 4 + b, src, :].astype(BF16)
        return c

    lax.fori_loop(0, 4, rim_low_half, 0)
    rim_b = remote(rim_s.at[1], rim_r.at[1], rim_ss.at[1], rim_rs.at[1], {"scan": right})
    rim_b.start()
    y_stage(7)

    def corner_out(i, c):
        rows = pl.ds(pl.multiple_of(i * 64, 64), 64)
        low = pl.ds(pl.multiple_of(512 + i * 64, 64), 64)
        for p in range(2):
            for b in range(2):
                lrim_s[0, p, b, rows, :] = grad[p, 4 + b, low, :].astype(BF16)
        return c

    lax.fori_loop(0, 4, corner_out, 0)
    crim_cp = remote(lrim_s.at[0], crim_r, rim_ss.at[0], rim_rs.at[0], {"obj": below})
    crim_cp.start()
    q_stage(6)
    gather(7, (0, 1, 2, 3))

    def low_out(i, c):
        rows = pl.ds(pl.multiple_of(i * 64, 64), 64)
        low = pl.ds(pl.multiple_of(512 + i * 64, 64), 64)
        for p in range(2):
            for b in range(4):
                lrim_s[1 + b // 2, p, b % 2, rows, :] = grad[p, b, low, :].astype(BF16)
        return c

    lax.fori_loop(0, 4, low_out, 0)
    lrim_cp = remote(lrim_s.at[pl.ds(1, 2)], lrim_r, rim_ss.at[2], rim_rs.at[2], {"obj": below})
    lrim_cp.start()
    out_cps = []
    for p in range(2):
        for b in range(4):
            cp = pltpu.make_async_copy(
                grad.at[p, b, pl.ds(0, 512)], out.at[p, :, pl.ds(b * 128, 128)], local_sem.at[p * 4 + b]
            )
            cp.start()
            out_cps.append(cp)
    crim_cp.wait_recv()

    def rim_top_half(i, c):
        rows = pl.ds(pl.multiple_of(i * 64, 64), 64)
        for p in range(2):
            for b in range(2):
                rim_s[0, p, b, rows, :] = (grad[p, 4 + b, rows, :] + crim_r[p, b, rows, :].astype(F32)).astype(BF16)
        return c

    lax.fori_loop(0, 4, rim_top_half, 0)
    rim_t = remote(rim_s.at[0], rim_r.at[0], rim_ss.at[3], rim_rs.at[3], {"scan": right})
    rim_t.start()
    q_stage(7)

    for code in range(4, 16):
        remote(q_s.at[0, 0], q_r.at[code], q_ss.at[code], q_rs.at[code], {"scan": right}).wait_recv()

    def x_copy(dx):
        return remote(x_s.at[dx], x_r.at[dx], x_ss.at[dx], x_rs.at[dx], {"scan": z * 4 + (x + 4 - dx) % 4})

    for dx in (1, 3, 2, 0):
        for p in range(2):
            total = q_r[dx, p].astype(F32)
            for dz in range(1, 4):
                total = total + q_r[dz * 4 + dx, p].astype(F32)
            x_s[dx, p] = total.astype(BF16)
        if dx:
            x_copy(dx).start()
    for dx in range(1, 4):
        x_copy(dx).wait_recv()
    piece = core * 4 + yy
    for p in range(2):
        total = x_s[0, p].astype(F32)
        for dx in range(1, 4):
            total = total + x_r[dx, p].astype(F32)
        g_s[p] = (total * (1.0 / 16.0)).astype(BF16)

    def g_copy(d):
        return remote(g_s, g_r.at[piece], g_ss.at[d - 1], g_rs.at[d - 1], {"obj": (band + d) % 8})

    for d in range(1, 8):
        g_copy(d).start()
    own_g = pltpu.make_async_copy(g_s, g_r.at[piece], local_sem.at[8])
    own_g.start()
    for d in range(1, 8):
        frm = (band + 8 - d) % 8
        at = frm % 2 * 4 + frm // 2
        remote(g_s, g_r.at[at], g_ss.at[d - 1], g_rs.at[d - 1], {"obj": frm}).wait_recv()
    for cp in (lrim_cp, rim_b, rim_t):
        cp.wait_recv()

    for cp in (*strip_cps, low_cp, corner_cp, crim_cp, rim_b, lrim_cp, rim_t):
        cp.wait_send()
    for t, s in sends:
        amp_copy(t, s).wait_send()

    def drain(i, c):
        sib_copy(i).wait_send()
        for d in range(1, 4):
            y_copy(i, d).wait_send()

        for a in range(2):

            @pl.when(owner_of(2 * i + a)[0] >= 4)
            def _():
                q_copy(i, a).wait_send()
        return c

    lax.fori_loop(0, 8, drain, 0)
    for d in range(1, 8):
        g_copy(d).wait_send()
    for dx in range(1, 4):
        x_copy(dx).wait_send()
    own_g.wait()
    for cp in out_cps:
        cp.wait()


def finish_kernel(main, rim, low, pieces, out, pout):
    out[...] = main[...]
    for b in range(2):
        for h in range(2):
            at = (0, slice(h * 256, h * 256 + 256), slice(b * 128, b * 128 + 128))
            out[at] = out[at] + rim[h, 0, b].astype(F32)
    for b in range(4):
        at = (0, slice(0, 256), slice(b * 128, b * 128 + 128))
        out[at] = out[at] + low[b // 2, 0, b % 2].astype(F32)
    for q in range(8):
        pout[0, 0, q * 32 : q * 32 + 32, :] = pieces[q, 0].astype(F32)


def on_device(object_field, probe, amplitudes, corner_row, corner_col):
    ltab, rtab = dft_tables(256)
    vm = pltpu.VMEM
    dma = pltpu.SemaphoreType.DMA
    anywhere = pl.BlockSpec(memory_space=pl.ANY)
    inside = pl.BlockSpec(memory_space=pltpu.VMEM)
    scalar = pl.BlockSpec(memory_space=pltpu.SMEM)
    main, rim, low, pieces = pl.pallas_call(
        kernel,
        out_shape=(
            jax.ShapeDtypeStruct((2, 512, 512), F32),
            jax.ShapeDtypeStruct((2, 2, 2, 256, 128), BF16),
            jax.ShapeDtypeStruct((2, 2, 2, 256, 128), BF16),
            jax.ShapeDtypeStruct((8, 2, 32, 256), BF16),
        ),
        in_specs=[scalar, scalar, anywhere, inside, anywhere, inside, inside],
        out_specs=(anywhere,) * 4,
        scratch_shapes=[
            vm((32, 256, 256), BF16),
            vm((2, 9, 768, 128), F32),
            vm((2, 6, 768, 128), F32),
            vm((25, 256 + 2 * RP, 128), F32),
            vm((4, 2, 256, 256), BF16),
            vm((4, 512, 256), BF16),
            vm((4, 256, 512), BF16),
            vm((4, 512, 256), BF16),
            vm((4, 256, 512), BF16),
            vm((8, 256, 512), F32),
            vm((2, 2, 256, 256), F32),
            vm((2, 2, 2, 256, 128), BF16),
            vm((2, 2, 2, 256, 128), BF16),
            vm((2, 4, 256, 128), BF16),
            vm((2, 4, 256, 128), BF16),
            vm((2, 2, 256, 128), BF16),
            vm((8, 2, 2, 128, 256), BF16),
            vm((8, 2, 2, 128, 256), BF16),
            vm((2, 2, 2, 128, 256), F32),
            vm((8, 4, 2, 2, 32, 256), BF16),
            vm((8, 3, 2, 2, 32, 256), BF16),
            vm((8, 2, 2, 32, 256), BF16),
            vm((16, 2, 32, 256), BF16),
            vm((4, 2, 32, 256), BF16),
            vm((4, 2, 32, 256), BF16),
            vm((2, 32, 256), BF16),
            vm((2, 2, 2, 256, 128), BF16),
            vm((3, 2, 2, 256, 128), BF16),
            vm((2, 2, 256, 128), BF16),
            dma((10,)),
            dma((4,)), dma((4,)),
            dma((32,)), dma((32,)),
            dma((8,)), dma((8,)),
            dma((24,)), dma((24,)),
            dma((16,)), dma((16,)),
            dma((4,)), dma((4,)),
            dma((7,)), dma((7,)),
            dma((4,)), dma((4,)),
        ],
        compiler_params=pltpu.CompilerParams(
            collective_id=0, has_side_effects=True, vmem_limit_bytes=62 * 2**20
        ),
        cost_estimate=pl.CostEstimate(flops=32 * 16 * 2 * 256**3, bytes_accessed=10 * 2**20, transcendentals=32 * 65536),
    )(
        corner_row[0].T, corner_col[0].T, object_field, probe, amplitudes[0],
        jnp.asarray(ltab), jnp.asarray(rtab),
    )
    return tuple(
        pl.pallas_call(
            finish_kernel,
            grid=(2,),
            in_specs=[
                pl.BlockSpec((1, 512, 512), lambda p: (p, 0, 0)),
                pl.BlockSpec((2, 1, 2, 256, 128), lambda p: (0, p, 0, 0, 0)),
                pl.BlockSpec((2, 1, 2, 256, 128), lambda p: (0, p, 0, 0, 0)),
                pl.BlockSpec((8, 1, 32, 256), lambda p: (0, p, 0, 0)),
            ],
            out_specs=(
                pl.BlockSpec((1, 512, 512), lambda p: (p, 0, 0)),
                pl.BlockSpec((1, 1, 256, 256), lambda p: (0, p, 0, 0)),
            ),
            out_shape=(
                jax.ShapeDtypeStruct((2, 512, 512), F32),
                jax.ShapeDtypeStruct((1, 2, 256, 256), F32),
            ),
            compiler_params=pltpu.CompilerParams(vmem_limit_bytes=60 * 2**20),
        )(main, rim, low, pieces)
    )


def solution(mesh):
    return jax.shard_map(
        on_device,
        mesh=mesh,
        in_specs=(
            P(None, "obj", "scan"),
            P(),
            P("obj", "scan", None, None),
            P("obj", "scan", None),
            P("obj", "scan", None),
        ),
        out_specs=(P(None, "obj", "scan"), P("scan", None, None, None)),
        check_vma=False,
    )
```

```python
import functools
import math

import jax
import jax.numpy as jnp
import ml_dtypes
import numpy as np
from jax import lax
from jax.experimental import pallas as pl
from jax.experimental.pallas import tpu as pltpu
from jax.sharding import PartitionSpec as P

MESH = pl.DeviceIdType.MESH
F32 = jnp.float32
BF16 = jnp.bfloat16

ORDER = [
    (0, 0), (1, 1), (3, 1), (1, 0), (3, 0), (0, 1), (2, 1), (1, 3),
    (3, 3), (1, 2), (3, 2), (0, 3), (2, 3), (2, 2), (0, 2), (2, 0),
]
CODES = [dz * 4 + dx for dz, dx in ORDER]
GROUPS = [(1, 2), (2, 4), (4, 6), (6, 8), (8, 10), (10, 12), (12, 14), (14, 16)]
RP = 32
CH = 32
EC = 32
PLAN = [
    ("X", 0), ("H", 0), ("X", 1), ("F", 0), ("H", 1), ("X", 2), ("F", 1), ("H", 2), ("X", 3), ("F", 2),
    ("H", 3), ("F", 3), ("A", 0), ("A", 1), ("A", 2), ("A", 3), ("D", 0), ("B", 0), ("D", 1), ("B", 1),
    ("D", 2), ("N", 0), ("B", 2), ("D", 3), ("N", 1), ("T", 0), ("B", 3), ("T", 1), ("N", 2), ("T", 2),
    ("N", 3), ("T", 3),
]


def dft_tables(length):
    grid = np.arange(length)
    angle = 2.0 * math.pi / length * (grid[:, None] * grid[None, :] % length)
    real = np.cos(angle) / math.sqrt(length)
    imag = -np.sin(angle) / math.sqrt(length)
    left = np.block([[real, -imag], [imag, real]])
    right = np.block([[real, imag], [-imag, real]])
    return left.astype(ml_dtypes.bfloat16), right.astype(ml_dtypes.bfloat16)


def code_of(n):
    return functools.reduce(lambda a, t: jnp.where(n == t, CODES[t], a), range(1, 16), jnp.int32(0))


def kernel(
    row_ref, col_ref, obj, probe, amps, ltab, rtab,
    out, rim_r, lrim_r, g_r,
    amp, ext, grad, term, patch, ebuf, hbuf, dbuf, bbuf, wide, pacc,
    strip_s, strip_r, low_s, low_r, corner_r,
    sib_s, sib_r, kept, y_s, y_r, q_s, q_r, x_s, x_r, g_s,
    rim_s, lrim_s, crim_r,
    local_sem, halo_ss, halo_rs, amp_ss, amp_rs, sib_ss, sib_rs, y_ss, y_rs, q_ss, q_rs, x_ss, x_rs, g_ss, g_rs, rim_ss, rim_rs,
):
    me = lax.axis_index("scan")
    band = lax.axis_index("obj")
    z, x = me // 4, me % 4
    yy, core = band // 2, band % 2
    left, right = (me + 15) % 16, (me + 1) % 16
    above, below = (band + 7) % 8, (band + 1) % 8

    barrier = pltpu.get_barrier_semaphore()
    for d in range(1, 16):
        pl.semaphore_signal(barrier, inc=1, device_id={"scan": (me + d) % 16}, device_id_type=MESH)
    for d in range(1, 8):
        pl.semaphore_signal(barrier, inc=1, device_id={"obj": (band + d) % 8}, device_id_type=MESH)

    def remote(src, dst, ss, rs, where):
        return pltpu.make_async_remote_copy(
            src_ref=src, dst_ref=dst, send_sem=ss, recv_sem=rs, device_id=where, device_id_type=MESH
        )

    tile_in = []
    for p in range(2):
        for b in range(4):
            cp = pltpu.make_async_copy(
                obj.at[p, :, pl.ds(b * 128, 128)], ext.at[p, b, pl.ds(0, 512)], local_sem.at[p * 4 + b]
            )
            cp.start()
            tile_in.append(cp)
    own_in = []
    for s in range(2):
        cp = pltpu.make_async_copy(amps.at[2 * me + s], amp.at[s * 16], local_sem.at[8 + s])
        cp.start()
        own_in.append(cp)
    pl.semaphore_wait(barrier, 22)

    def amp_copy(t, s):
        dz, dx = ORDER[t]
        target = ((z + dz) % 4) * 4 + (x + dx) % 4
        at = s * 16 + CODES[t]
        return remote(amps.at[2 * target + s], amp.at[at], amp_ss.at[at], amp_rs.at[at], {"scan": target})

    sends = [(t, s) for g, e in GROUPS for s in range(2) for t in range(g, e)]
    for t, s in sends[:6]:
        amp_copy(t, s).start()
    for cp in tile_in:
        cp.wait()

    def round_rows(i, c):
        rows = pl.ds(pl.multiple_of(i * 64, 64), 64)
        for p in range(2):
            for b in range(4):
                v = ext[p, b, rows, :].astype(BF16)
                ext[p, b, rows, :] = v.astype(F32)
                if b < 2:
                    strip_s[i // 4, p, b, pl.ds(pl.multiple_of(i % 4 * 64, 64), 64), :] = v
        return c

    lax.fori_loop(0, 8, round_rows, 0)

    def low_rows(i, c):
        rows = pl.ds(pl.multiple_of(i * 64, 64), 64)
        for p in range(2):
            for b in range(4):
                low_s[p, b, rows, :] = ext[p, b, rows, :].astype(BF16)
        return c

    lax.fori_loop(0, 4, low_rows, 0)

    strip_cps = [
        remote(strip_s.at[h], strip_r.at[h], halo_ss.at[3 * h], halo_rs.at[3 * h], {"scan": left}) for h in range(2)
    ]
    for cp in strip_cps:
        cp.start()
    low_cp = remote(low_s, low_r, halo_ss.at[1], halo_rs.at[1], {"obj": above})
    low_cp.start()

    for t, s in sends[6:]:
        amp_copy(t, s).start()

    def zero_rows(i, c):
        rows = pl.ds(pl.multiple_of(i * 64, 64), 64)
        nil = jnp.zeros((64, 128), F32)
        for p in range(2):
            for b in range(3):
                ext[p, 6 + b, rows, :] = nil
            for b in range(6):
                grad[p, b, rows, :] = nil
        return c

    lax.fori_loop(0, 12, zero_rows, 0)

    def zero_terms(i, c):
        nil = jnp.zeros((RP, 128), F32)
        term[i, 0:RP, :] = nil
        term[i, RP + 256 : RP + 256 + RP, :] = nil
        return c

    lax.fori_loop(0, 24, zero_terms, 0)
    term[24] = jnp.zeros((256 + 2 * RP, 128), F32)

    strip_cps[0].wait_recv()
    corner_cp = remote(strip_r.at[0], corner_r, halo_ss.at[2], halo_rs.at[2], {"obj": above})
    corner_cp.start()

    def strip_rows(h):
        def rows_of(i, c):
            rows = pl.ds(pl.multiple_of(i * 64, 64), 64)
            dest = pl.ds(pl.multiple_of(h * 256 + i * 64, 64), 64)
            for p in range(2):
                for b in range(2):
                    ext[p, 4 + b, dest, :] = strip_r[h, p, b, rows, :].astype(F32)
            return c

        lax.fori_loop(0, 4, rows_of, 0)

    strip_rows(0)
    low_cp.wait_recv()

    def low_in(i, c):
        rows = pl.ds(pl.multiple_of(i * 64, 64), 64)
        dest = pl.ds(pl.multiple_of(512 + i * 64, 64), 64)
        for p in range(2):
            for b in range(4):
                ext[p, b, dest, :] = low_r[p, b, rows, :].astype(F32)
        return c

    lax.fori_loop(0, 4, low_in, 0)
    strip_cps[1].wait_recv()
    strip_rows(1)
    corner_cp.wait_recv()

    def corner_in(i, c):
        rows = pl.ds(pl.multiple_of(i * 64, 64), 64)
        dest = pl.ds(pl.multiple_of(512 + i * 64, 64), 64)
        for p in range(2):
            for b in range(2):
                ext[p, 4 + b, dest, :] = corner_r[p, b, rows, :].astype(F32)
        return c

    lax.fori_loop(0, 4, corner_in, 0)
    for cp in own_in:
        cp.wait()

    lane = lax.broadcasted_iota(jnp.int32, (EC, 128), 1)

    def owner_of(n):
        code = code_of(n)
        dz, dx = code // 4, code % 4
        return code, ((z + 4 - dz) % 4) * 4 + (x + 4 - dx) % 4

    def amp_wait(at):
        pltpu.make_async_remote_copy(
            src_ref=amp.at[at], dst_ref=amp.at[at], send_sem=amp_ss.at[at], recv_sem=amp_rs.at[at],
            device_id={"scan": right}, device_id_type=MESH,
        ).wait_recv()

    def four(v):
        slots = []
        for a in range(2):
            code, owner = owner_of(2 * v + a)
            for s in range(2):
                at = s * 16 + code
                row = row_ref[s, owner]
                col = col_ref[s, owner]
                c0 = jnp.maximum(col, 0)
                slots.append((at, jnp.maximum(row, 0), jnp.where(row >= 0, c0 // 128, 6), c0 % 128))

        def arrived(k):
            if k < 2:
                pl.when(v > 0)(functools.partial(amp_wait, slots[k][0]))
            else:
                amp_wait(slots[k][0])

        def exit_wave(k):
            at, r0, block, shift = slots[k]
            for rc in range(0, 256, EC):
                rows = slice(rc, rc + EC)
                f = []
                for p in range(2):
                    raw = [ext[p, block + q, pl.ds(r0 + rc, EC), :] for q in range(3)]
                    f.append([
                        pltpu.roll(jnp.where(lane >= shift, raw[b], raw[b + 1]).astype(BF16), (128 - shift) % 128, 1)
                        for b in range(2)
                    ])
                for b in range(2):
                    lanes = slice(b * 128, b * 128 + 128)
                    fr, fi = f[0][b].astype(F32), f[1][b].astype(F32)
                    pr, pi = probe[0, rows, lanes], probe[1, rows, lanes]
                    patch[k, 0, rows, lanes] = f[0][b]
                    patch[k, 1, rows, lanes] = f[1][b]
                    ebuf[k, rows, lanes] = (pr * fr - pi * fi).astype(BF16)
                    ebuf[k, 256 + rc : 256 + rc + EC, lanes] = (pr * fi + pi * fr).astype(BF16)

        def half_to(k):
            h = jnp.dot(ltab[...], ebuf[k], preferred_element_type=F32).astype(BF16)
            hbuf[k, :, 0:256] = h[0:256]
            hbuf[k, :, 256:512] = h[256:512]

        def far_to(k):
            wide[k] = jnp.dot(hbuf[k], rtab[...], preferred_element_type=F32)

        def differ(k):
            at = slots[k][0]
            for rc in range(0, 256, EC):
                rows = slice(rc, rc + EC)
                fr, fi = wide[k, rows, 0:256], wide[k, rows, 256:512]
                m = amp[at, rows, :].astype(F32)
                scale = m * lax.rsqrt(jnp.maximum(fr * fr + fi * fi, 0.01)) - 1.0
                dbuf[k, rows, :] = (fr * scale).astype(BF16)
                dbuf[k, 256 + rc : 256 + rc + EC, :] = (fi * scale).astype(BF16)

        def back_to(k):
            h = jnp.dot(rtab[...], dbuf[k], preferred_element_type=F32).astype(BF16)
            bbuf[k, :, 0:256] = h[0:256]
            bbuf[k, :, 256:512] = h[256:512]

        def near_to(k):
            wide[4 + k] = jnp.dot(bbuf[k], ltab[...], preferred_element_type=F32)

        def terms(k):
            at, r0, block, shift = slots[k]
            n, second = k // 2, k % 2 == 1
            for rc in range(0, 256, EC):
                rows = slice(rc, rc + EC)
                trail = [None, None]
                for b in range(2):
                    lanes = slice(b * 128, b * 128 + 128)
                    nr = wide[4 + k, rows, b * 128 : b * 128 + 128]
                    ni = wide[4 + k, rows, 256 + b * 128 : 256 + b * 128 + 128]
                    pr, pi = probe[0, rows, lanes], probe[1, rows, lanes]
                    fr, fi = patch[k, 0, rows, lanes].astype(F32), patch[k, 1, rows, lanes].astype(F32)
                    tt = (pr * nr + pi * ni, pr * ni - pi * nr)
                    for p in range(2):
                        turned = pltpu.roll(tt[p].astype(BF16), shift, 1).astype(F32)
                        before = trail[p] if b else jnp.zeros_like(turned)
                        term[k * 6 + p * 3 + b, RP + rc : RP + rc + EC, :] = jnp.where(lane >= shift, turned, before)
                        trail[p] = turned
                    pt = (fr * nr + fi * ni, fr * ni - fi * nr)
                    for p in range(2):
                        pacc[n, p, rows, lanes] = pacc[n, p, rows, lanes] + pt[p] if second else pt[p]
                for p in range(2):
                    term[k * 6 + p * 3 + 2, RP + rc : RP + rc + EC, :] = jnp.where(
                        lane >= shift, jnp.zeros_like(trail[p]), trail[p]
                    )

        stages = {"A": arrived, "X": exit_wave, "H": half_to, "F": far_to, "D": differ, "B": back_to, "N": near_to, "T": terms}
        for stage, k in PLAN:
            stages[stage](k)

    def gather(v, blocks):
        places = []
        for w in range(4):
            code, owner = owner_of(2 * v + w // 2)
            row = jnp.maximum(row_ref[w % 2, owner], 0)
            block = jnp.maximum(col_ref[w % 2, owner], 0) // 128
            places.append((row, block))
        picks = [
            [
                [
                    jnp.where((b - block >= 0) & (b - block < 3), w * 6 + p * 3 + b - block, 24)
                    for w, (row, block) in enumerate(places)
                ]
                for b in range(6)
            ]
            for p in range(2)
        ]

        def rows_of(ic, c):
            rows = pl.ds(pl.multiple_of(ic * CH, CH), CH)
            starts = [jnp.clip(ic * CH - row, -RP, 256) + RP for row, block in places]
            for b in blocks:
                for p in range(2):
                    acc = grad[p, b, rows, :]
                    for w in range(4):
                        acc = acc + term[picks[p][b][w], pl.ds(starts[w], CH), :]
                    grad[p, b, rows, :] = acc
            return c

        lax.fori_loop(0, 768 // CH, rows_of, 0)

    def sib_copy(i):
        return remote(sib_s.at[i], sib_r.at[i], sib_ss.at[i], sib_rs.at[i], {"obj": 2 * yy + 1 - core})

    def y_copy(i, d):
        to = (yy + d) % 4
        return remote(
            y_s.at[i, to], y_r.at[i, d - 1], y_ss.at[i * 3 + d - 1], y_rs.at[i * 3 + d - 1], {"obj": 2 * to + core}
        )

    def q_copy(i, a):
        code, owner = owner_of(2 * i + a)
        return remote(q_s.at[i, a], q_r.at[code], q_ss.at[code], q_rs.at[code], {"scan": owner // 4 * 4 + x})

    mine = pl.ds(pl.multiple_of(core * 128, 128), 128)
    other = pl.ds(pl.multiple_of((1 - core) * 128, 128), 128)

    def sib_stage(i):
        for a in range(2):
            for p in range(2):
                sib_s[i, a, p] = pacc[a, p, other, :].astype(BF16)
                kept[i % 2, a, p] = pacc[a, p, mine, :]
        sib_copy(i).start()

    def y_stage(i):
        sib_copy(i).wait_recv()
        for a in range(2):
            for p in range(2):
                total = kept[i % 2, a, p] + sib_r[i, a, p].astype(F32)
                for q in range(4):
                    y_s[i, q, a, p] = total[q * 32 : q * 32 + 32].astype(BF16)
        for d in range(1, 4):
            y_copy(i, d).start()

    def q_stage(i):
        for d in range(1, 4):
            y_copy(i, d).wait_recv()
        for a in range(2):
            for p in range(2):
                total = y_s[i, yy, a, p].astype(F32)
                for d in range(3):
                    total = total + y_r[i, d, a, p].astype(F32)
                q_s[i, a, p] = total.astype(BF16)

        for a in range(2):
            code, owner = owner_of(2 * i + a)

            @pl.when(code >= 4)
            def _():
                q_copy(i, a).start()

            @pl.when(code < 4)
            def _():
                q_r[code] = q_s[i, a]

    def step(v, c):
        @pl.when(v >= 1)
        def _():
            y_stage(v - 1)

        @pl.when(v >= 2)
        def _():
            q_stage(v - 2)

        four(v)
        sib_stage(v)
        gather(v, (4, 5))

        @pl.when(v < 7)
        def _():
            gather(v, (0, 1, 2, 3))

        return c

    lax.fori_loop(0, 8, step, 0)

    def rim_low_half(i, c):
        rows = pl.ds(pl.multiple_of(i * 64, 64), 64)
        src = pl.ds(pl.multiple_of(256 + i * 64, 64), 64)
        for p in range(2):
            for b in range(2):
                rim_s[1, p, b, rows, :] = grad[p, 4 + b, src, :].astype(BF16)
        return c

    lax.fori_loop(0, 4, rim_low_half, 0)
    rim_b = remote(rim_s.at[1], rim_r.at[1], rim_ss.at[1], rim_rs.at[1], {"scan": right})
    rim_b.start()
    y_stage(7)

    def corner_out(i, c):
        rows = pl.ds(pl.multiple_of(i * 64, 64), 64)
        low = pl.ds(pl.multiple_of(512 + i * 64, 64), 64)
        for p in range(2):
            for b in range(2):
                lrim_s[0, p, b, rows, :] = grad[p, 4 + b, low, :].astype(BF16)
        return c

    lax.fori_loop(0, 4, corner_out, 0)
    crim_cp = remote(lrim_s.at[0], crim_r, rim_ss.at[0], rim_rs.at[0], {"obj": below})
    crim_cp.start()
    q_stage(6)
    gather(7, (0, 1, 2, 3))

    def low_out(i, c):
        rows = pl.ds(pl.multiple_of(i * 64, 64), 64)
        low = pl.ds(pl.multiple_of(512 + i * 64, 64), 64)
        for p in range(2):
            for b in range(4):
                lrim_s[1 + b // 2, p, b % 2, rows, :] = grad[p, b, low, :].astype(BF16)
        return c

    lax.fori_loop(0, 4, low_out, 0)
    lrim_cp = remote(lrim_s.at[pl.ds(1, 2)], lrim_r, rim_ss.at[2], rim_rs.at[2], {"obj": below})
    lrim_cp.start()
    out_cps = []
    for p in range(2):
        for b in range(4):
            cp = pltpu.make_async_copy(
                grad.at[p, b, pl.ds(0, 512)], out.at[p, :, pl.ds(b * 128, 128)], local_sem.at[p * 4 + b]
            )
            cp.start()
            out_cps.append(cp)
    crim_cp.wait_recv()

    def rim_top_half(i, c):
        rows = pl.ds(pl.multiple_of(i * 64, 64), 64)
        for p in range(2):
            for b in range(2):
                rim_s[0, p, b, rows, :] = (grad[p, 4 + b, rows, :] + crim_r[p, b, rows, :].astype(F32)).astype(BF16)
        return c

    lax.fori_loop(0, 4, rim_top_half, 0)
    rim_t = remote(rim_s.at[0], rim_r.at[0], rim_ss.at[3], rim_rs.at[3], {"scan": right})
    rim_t.start()
    q_stage(7)

    for code in range(4, 16):
        remote(q_s.at[0, 0], q_r.at[code], q_ss.at[code], q_rs.at[code], {"scan": right}).wait_recv()

    def x_copy(dx):
        return remote(x_s.at[dx], x_r.at[dx], x_ss.at[dx], x_rs.at[dx], {"scan": z * 4 + (x + 4 - dx) % 4})

    for dx in (1, 3, 2, 0):
        for p in range(2):
            total = q_r[dx, p].astype(F32)
            for dz in range(1, 4):
                total = total + q_r[dz * 4 + dx, p].astype(F32)
            x_s[dx, p] = total.astype(BF16)
        if dx:
            x_copy(dx).start()
    for dx in range(1, 4):
        x_copy(dx).wait_recv()
    piece = core * 4 + yy
    for p in range(2):
        total = x_s[0, p].astype(F32)
        for dx in range(1, 4):
            total = total + x_r[dx, p].astype(F32)
        g_s[p] = (total * (1.0 / 16.0)).astype(BF16)

    def g_copy(d):
        return remote(g_s, g_r.at[piece], g_ss.at[d - 1], g_rs.at[d - 1], {"obj": (band + d) % 8})

    for d in range(1, 8):
        g_copy(d).start()
    own_g = pltpu.make_async_copy(g_s, g_r.at[piece], local_sem.at[8])
    own_g.start()
    for d in range(1, 8):
        frm = (band + 8 - d) % 8
        at = frm % 2 * 4 + frm // 2
        remote(g_s, g_r.at[at], g_ss.at[d - 1], g_rs.at[d - 1], {"obj": frm}).wait_recv()
    for cp in (lrim_cp, rim_b, rim_t):
        cp.wait_recv()

    for cp in (*strip_cps, low_cp, corner_cp, crim_cp, rim_b, lrim_cp, rim_t):
        cp.wait_send()
    for t, s in sends:
        amp_copy(t, s).wait_send()

    def drain(i, c):
        sib_copy(i).wait_send()
        for d in range(1, 4):
            y_copy(i, d).wait_send()

        for a in range(2):

            @pl.when(owner_of(2 * i + a)[0] >= 4)
            def _():
                q_copy(i, a).wait_send()
        return c

    lax.fori_loop(0, 8, drain, 0)
    for d in range(1, 8):
        g_copy(d).wait_send()
    for dx in range(1, 4):
        x_copy(dx).wait_send()
    own_g.wait()
    for cp in out_cps:
        cp.wait()


def finish_kernel(main, rim, low, pieces, out, pout):
    out[...] = main[...]
    for b in range(2):
        for h in range(2):
            at = (0, slice(h * 256, h * 256 + 256), slice(b * 128, b * 128 + 128))
            out[at] = out[at] + rim[h, 0, b].astype(F32)
    for b in range(4):
        at = (0, slice(0, 256), slice(b * 128, b * 128 + 128))
        out[at] = out[at] + low[b // 2, 0, b % 2].astype(F32)
    for q in range(8):
        pout[0, 0, q * 32 : q * 32 + 32, :] = pieces[q, 0].astype(F32)


def on_device(object_field, probe, amplitudes, corner_row, corner_col):
    ltab, rtab = dft_tables(256)
    vm = pltpu.VMEM
    dma = pltpu.SemaphoreType.DMA
    anywhere = pl.BlockSpec(memory_space=pl.ANY)
    inside = pl.BlockSpec(memory_space=pltpu.VMEM)
    scalar = pl.BlockSpec(memory_space=pltpu.SMEM)
    main, rim, low, pieces = pl.pallas_call(
        kernel,
        out_shape=(
            jax.ShapeDtypeStruct((2, 512, 512), F32),
            jax.ShapeDtypeStruct((2, 2, 2, 256, 128), BF16),
            jax.ShapeDtypeStruct((2, 2, 2, 256, 128), BF16),
            jax.ShapeDtypeStruct((8, 2, 32, 256), BF16),
        ),
        in_specs=[scalar, scalar, anywhere, inside, anywhere, inside, inside],
        out_specs=(anywhere,) * 4,
        scratch_shapes=[
            vm((32, 256, 256), BF16),
            vm((2, 9, 768, 128), F32),
            vm((2, 6, 768, 128), F32),
            vm((25, 256 + 2 * RP, 128), F32),
            vm((4, 2, 256, 256), BF16),
            vm((4, 512, 256), BF16),
            vm((4, 256, 512), BF16),
            vm((4, 512, 256), BF16),
            vm((4, 256, 512), BF16),
            vm((8, 256, 512), F32),
            vm((2, 2, 256, 256), F32),
            vm((2, 2, 2, 256, 128), BF16),
            vm((2, 2, 2, 256, 128), BF16),
            vm((2, 4, 256, 128), BF16),
            vm((2, 4, 256, 128), BF16),
            vm((2, 2, 256, 128), BF16),
            vm((8, 2, 2, 128, 256), BF16),
            vm((8, 2, 2, 128, 256), BF16),
            vm((2, 2, 2, 128, 256), F32),
            vm((8, 4, 2, 2, 32, 256), BF16),
            vm((8, 3, 2, 2, 32, 256), BF16),
            vm((8, 2, 2, 32, 256), BF16),
            vm((16, 2, 32, 256), BF16),
            vm((4, 2, 32, 256), BF16),
            vm((4, 2, 32, 256), BF16),
            vm((2, 32, 256), BF16),
            vm((2, 2, 2, 256, 128), BF16),
            vm((3, 2, 2, 256, 128), BF16),
            vm((2, 2, 256, 128), BF16),
            dma((10,)),
            dma((4,)), dma((4,)),
            dma((32,)), dma((32,)),
            dma((8,)), dma((8,)),
            dma((24,)), dma((24,)),
            dma((16,)), dma((16,)),
            dma((4,)), dma((4,)),
            dma((7,)), dma((7,)),
            dma((4,)), dma((4,)),
        ],
        compiler_params=pltpu.CompilerParams(
            collective_id=0, has_side_effects=True, vmem_limit_bytes=62 * 2**20
        ),
        cost_estimate=pl.CostEstimate(flops=32 * 16 * 2 * 256**3, bytes_accessed=10 * 2**20, transcendentals=32 * 65536),
    )(
        corner_row[0].T, corner_col[0].T, object_field, probe, amplitudes[0],
        jnp.asarray(ltab), jnp.asarray(rtab),
    )
    return tuple(
        pl.pallas_call(
            finish_kernel,
            grid=(2,),
            in_specs=[
                pl.BlockSpec((1, 512, 512), lambda p: (p, 0, 0)),
                pl.BlockSpec((2, 1, 2, 256, 128), lambda p: (0, p, 0, 0, 0)),
                pl.BlockSpec((2, 1, 2, 256, 128), lambda p: (0, p, 0, 0, 0)),
                pl.BlockSpec((8, 1, 32, 256), lambda p: (0, p, 0, 0)),
            ],
            out_specs=(
                pl.BlockSpec((1, 512, 512), lambda p: (p, 0, 0)),
                pl.BlockSpec((1, 1, 256, 256), lambda p: (0, p, 0, 0)),
            ),
            out_shape=(
                jax.ShapeDtypeStruct((2, 512, 512), F32),
                jax.ShapeDtypeStruct((1, 2, 256, 256), F32),
            ),
            compiler_params=pltpu.CompilerParams(vmem_limit_bytes=60 * 2**20),
        )(main, rim, low, pieces)
    )


def solution(mesh):
    return jax.shard_map(
        on_device,
        mesh=mesh,
        in_specs=(
            P(None, "obj", "scan"),
            P(),
            P("obj", "scan", None, None),
            P("obj", "scan", None),
            P("obj", "scan", None),
        ),
        out_specs=(P(None, "obj", "scan"), P("scan", None, None, None)),
        check_vma=False,
    )
```

```python
import functools
import math

import jax
import jax.numpy as jnp
import ml_dtypes
import numpy as np
from jax import lax
from jax.experimental import pallas as pl
from jax.experimental.pallas import tpu as pltpu
from jax.sharding import PartitionSpec as P

MESH = pl.DeviceIdType.MESH
F32 = jnp.float32
BF16 = jnp.bfloat16

ORDER = [
    (0, 0), (1, 1), (3, 1), (1, 0), (3, 0), (0, 1), (2, 1), (1, 3),
    (3, 3), (1, 2), (3, 2), (0, 3), (2, 3), (2, 2), (0, 2), (2, 0),
]
CODES = [dz * 4 + dx for dz, dx in ORDER]
GROUPS = [(1, 2), (2, 4), (4, 6), (6, 8), (8, 10), (10, 12), (12, 14), (14, 16)]
RP = 32
CH = 32
EC = 32
PLAN = [
    ("X", 0), ("H", 0), ("X", 1), ("F", 0), ("H", 1), ("X", 2), ("F", 1), ("H", 2), ("X", 3), ("F", 2),
    ("H", 3), ("F", 3), ("A", 0), ("A", 1), ("A", 2), ("A", 3), ("D", 0), ("B", 0), ("D", 1), ("B", 1),
    ("D", 2), ("N", 0), ("B", 2), ("D", 3), ("N", 1), ("T", 0), ("B", 3), ("T", 1), ("N", 2), ("T", 2),
    ("N", 3), ("T", 3),
]


def dft_tables(length):
    grid = np.arange(length)
    angle = 2.0 * math.pi / length * (grid[:, None] * grid[None, :] % length)
    real = np.cos(angle) / math.sqrt(length)
    imag = -np.sin(angle) / math.sqrt(length)
    left = np.block([[real, -imag], [imag, real]])
    right = np.block([[real, imag], [-imag, real]])
    return left.astype(ml_dtypes.bfloat16), right.astype(ml_dtypes.bfloat16)


def code_of(n):
    return functools.reduce(lambda a, t: jnp.where(n == t, CODES[t], a), range(1, 16), jnp.int32(0))


def kernel(
    row_ref, col_ref, obj, probe, amps, ltab, rtab,
    out, rim_r, lrim_r, g_r,
    amp, ext, grad, term, patch, ebuf, hbuf, dbuf, bbuf, wide, pacc,
    strip_s, strip_r, low_s, low_r, corner_r,
    sib_s, sib_r, kept, y_s, y_r, q_s, q_r, x_s, x_r, g_s,
    rim_s, lrim_s, crim_r,
    local_sem, halo_ss, halo_rs, amp_ss, amp_rs, sib_ss, sib_rs, y_ss, y_rs, q_ss, q_rs, x_ss, x_rs, g_ss, g_rs, rim_ss, rim_rs,
):
    me = lax.axis_index("scan")
    band = lax.axis_index("obj")
    z, x = me // 4, me % 4
    yy, core = band // 2, band % 2
    left, right = (me + 15) % 16, (me + 1) % 16
    above, below = (band + 7) % 8, (band + 1) % 8

    barrier = pltpu.get_barrier_semaphore()
    for d in range(1, 16):
        pl.semaphore_signal(barrier, inc=1, device_id={"scan": (me + d) % 16}, device_id_type=MESH)
    for d in range(1, 8):
        pl.semaphore_signal(barrier, inc=1, device_id={"obj": (band + d) % 8}, device_id_type=MESH)

    def remote(src, dst, ss, rs, where):
        return pltpu.make_async_remote_copy(
            src_ref=src, dst_ref=dst, send_sem=ss, recv_sem=rs, device_id=where, device_id_type=MESH
        )

    tile_in = []
    for p in range(2):
        for b in range(4):
            cp = pltpu.make_async_copy(
                obj.at[p, :, pl.ds(b * 128, 128)], ext.at[p, b, pl.ds(0, 512)], local_sem.at[p * 4 + b]
            )
            cp.start()
            tile_in.append(cp)
    own_in = []
    for s in range(2):
        cp = pltpu.make_async_copy(amps.at[2 * me + s], amp.at[s * 16], local_sem.at[8 + s])
        cp.start()
        own_in.append(cp)
    pl.semaphore_wait(barrier, 22)

    def amp_copy(t, s):
        dz, dx = ORDER[t]
        target = ((z + dz) % 4) * 4 + (x + dx) % 4
        at = s * 16 + CODES[t]
        return remote(amps.at[2 * target + s], amp.at[at], amp_ss.at[at], amp_rs.at[at], {"scan": target})

    sends = [(t, s) for g, e in GROUPS for s in range(2) for t in range(g, e)]
    for t, s in sends[:6]:
        amp_copy(t, s).start()
    for cp in tile_in:
        cp.wait()

    def round_rows(i, c):
        rows = pl.ds(pl.multiple_of(i * 64, 64), 64)
        for p in range(2):
            for b in range(4):
                v = ext[p, b, rows, :].astype(BF16)
                ext[p, b, rows, :] = v.astype(F32)
                if b < 2:
                    strip_s[i // 4, p, b, pl.ds(pl.multiple_of(i % 4 * 64, 64), 64), :] = v
        return c

    lax.fori_loop(0, 8, round_rows, 0)

    def low_rows(i, c):
        rows = pl.ds(pl.multiple_of(i * 64, 64), 64)
        for p in range(2):
            for b in range(4):
                low_s[p, b, rows, :] = ext[p, b, rows, :].astype(BF16)
        return c

    lax.fori_loop(0, 4, low_rows, 0)

    strip_cps = [
        remote(strip_s.at[h], strip_r.at[h], halo_ss.at[3 * h], halo_rs.at[3 * h], {"scan": left}) for h in range(2)
    ]
    for cp in strip_cps:
        cp.start()
    low_cp = remote(low_s, low_r, halo_ss.at[1], halo_rs.at[1], {"obj": above})
    low_cp.start()

    for t, s in sends[6:]:
        amp_copy(t, s).start()

    def zero_rows(i, c):
        rows = pl.ds(pl.multiple_of(i * 64, 64), 64)
        nil = jnp.zeros((64, 128), F32)
        for p in range(2):
            for b in range(3):
                ext[p, 6 + b, rows, :] = nil
            for b in range(6):
                grad[p, b, rows, :] = nil
        return c

    lax.fori_loop(0, 12, zero_rows, 0)

    def zero_terms(i, c):
        nil = jnp.zeros((RP, 128), F32)
        term[i, 0:RP, :] = nil
        term[i, RP + 256 : RP + 256 + RP, :] = nil
        return c

    lax.fori_loop(0, 24, zero_terms, 0)
    term[24] = jnp.zeros((256 + 2 * RP, 128), F32)

    strip_cps[0].wait_recv()
    corner_cp = remote(strip_r.at[0], corner_r, halo_ss.at[2], halo_rs.at[2], {"obj": above})
    corner_cp.start()

    def strip_rows(h):
        def rows_of(i, c):
            rows = pl.ds(pl.multiple_of(i * 64, 64), 64)
            dest = pl.ds(pl.multiple_of(h * 256 + i * 64, 64), 64)
            for p in range(2):
                for b in range(2):
                    ext[p, 4 + b, dest, :] = strip_r[h, p, b, rows, :].astype(F32)
            return c

        lax.fori_loop(0, 4, rows_of, 0)

    strip_rows(0)
    low_cp.wait_recv()

    def low_in(i, c):
        rows = pl.ds(pl.multiple_of(i * 64, 64), 64)
        dest = pl.ds(pl.multiple_of(512 + i * 64, 64), 64)
        for p in range(2):
            for b in range(4):
                ext[p, b, dest, :] = low_r[p, b, rows, :].astype(F32)
        return c

    lax.fori_loop(0, 4, low_in, 0)
    strip_cps[1].wait_recv()
    strip_rows(1)
    corner_cp.wait_recv()

    def corner_in(i, c):
        rows = pl.ds(pl.multiple_of(i * 64, 64), 64)
        dest = pl.ds(pl.multiple_of(512 + i * 64, 64), 64)
        for p in range(2):
            for b in range(2):
                ext[p, 4 + b, dest, :] = corner_r[p, b, rows, :].astype(F32)
        return c

    lax.fori_loop(0, 4, corner_in, 0)
    for cp in own_in:
        cp.wait()

    lane = lax.broadcasted_iota(jnp.int32, (EC, 128), 1)

    def owner_of(n):
        code = code_of(n)
        dz, dx = code // 4, code % 4
        return code, ((z + 4 - dz) % 4) * 4 + (x + 4 - dx) % 4

    def amp_wait(at):
        pltpu.make_async_remote_copy(
            src_ref=amp.at[at], dst_ref=amp.at[at], send_sem=amp_ss.at[at], recv_sem=amp_rs.at[at],
            device_id={"scan": right}, device_id_type=MESH,
        ).wait_recv()

    def four(v):
        slots = []
        for a in range(2):
            code, owner = owner_of(2 * v + a)
            for s in range(2):
                at = s * 16 + code
                row = row_ref[s, owner]
                col = col_ref[s, owner]
                c0 = jnp.maximum(col, 0)
                slots.append((at, jnp.maximum(row, 0), jnp.where(row >= 0, c0 // 128, 6), c0 % 128))

        def arrived(k):
            if k < 2:
                pl.when(v > 0)(functools.partial(amp_wait, slots[k][0]))
            else:
                amp_wait(slots[k][0])

        def exit_wave(k):
            at, r0, block, shift = slots[k]
            for rc in range(0, 256, EC):
                rows = slice(rc, rc + EC)
                f = []
                for p in range(2):
                    raw = [ext[p, block + q, pl.ds(r0 + rc, EC), :] for q in range(3)]
                    f.append([
                        pltpu.roll(jnp.where(lane >= shift, raw[b], raw[b + 1]).astype(BF16), (128 - shift) % 128, 1)
                        for b in range(2)
                    ])
                for b in range(2):
                    lanes = slice(b * 128, b * 128 + 128)
                    fr, fi = f[0][b].astype(F32), f[1][b].astype(F32)
                    pr, pi = probe[0, rows, lanes], probe[1, rows, lanes]
                    patch[k, 0, rows, lanes] = f[0][b]
                    patch[k, 1, rows, lanes] = f[1][b]
                    ebuf[k, rows, lanes] = (pr * fr - pi * fi).astype(BF16)
                    ebuf[k, 256 + rc : 256 + rc + EC, lanes] = (pr * fi + pi * fr).astype(BF16)

        def half_to(k):
            h = jnp.dot(ltab[...], ebuf[k], preferred_element_type=F32).astype(BF16)
            hbuf[k, :, 0:256] = h[0:256]
            hbuf[k, :, 256:512] = h[256:512]

        def far_to(k):
            wide[k] = jnp.dot(hbuf[k], rtab[...], preferred_element_type=F32)

        def differ(k):
            at = slots[k][0]
            for rc in range(0, 256, EC):
                rows = slice(rc, rc + EC)
                fr, fi = wide[k, rows, 0:256], wide[k, rows, 256:512]
                m = amp[at, rows, :].astype(F32)
                scale = m * lax.rsqrt(jnp.maximum(fr * fr + fi * fi, 0.01)) - 1.0
                dbuf[k, rows, :] = (fr * scale).astype(BF16)
                dbuf[k, 256 + rc : 256 + rc + EC, :] = (fi * scale).astype(BF16)

        def back_to(k):
            h = jnp.dot(rtab[...], dbuf[k], preferred_element_type=F32).astype(BF16)
            bbuf[k, :, 0:256] = h[0:256]
            bbuf[k, :, 256:512] = h[256:512]

        def near_to(k):
            wide[4 + k] = jnp.dot(bbuf[k], ltab[...], preferred_element_type=F32)

        def terms(k):
            at, r0, block, shift = slots[k]
            n, second = k // 2, k % 2 == 1
            for rc in range(0, 256, EC):
                rows = slice(rc, rc + EC)
                trail = [None, None]
                for b in range(2):
                    lanes = slice(b * 128, b * 128 + 128)
                    nr = wide[4 + k, rows, b * 128 : b * 128 + 128]
                    ni = wide[4 + k, rows, 256 + b * 128 : 256 + b * 128 + 128]
                    pr, pi = probe[0, rows, lanes], probe[1, rows, lanes]
                    fr, fi = patch[k, 0, rows, lanes].astype(F32), patch[k, 1, rows, lanes].astype(F32)
                    tt = (pr * nr + pi * ni, pr * ni - pi * nr)
                    for p in range(2):
                        turned = pltpu.roll(tt[p].astype(BF16), shift, 1).astype(F32)
                        before = trail[p] if b else jnp.zeros_like(turned)
                        term[k * 6 + p * 3 + b, RP + rc : RP + rc + EC, :] = jnp.where(lane >= shift, turned, before)
                        trail[p] = turned
                    pt = (fr * nr + fi * ni, fr * ni - fi * nr)
                    for p in range(2):
                        pacc[n, p, rows, lanes] = pacc[n, p, rows, lanes] + pt[p] if second else pt[p]
                for p in range(2):
                    term[k * 6 + p * 3 + 2, RP + rc : RP + rc + EC, :] = jnp.where(
                        lane >= shift, jnp.zeros_like(trail[p]), trail[p]
                    )

        stages = {"A": arrived, "X": exit_wave, "H": half_to, "F": far_to, "D": differ, "B": back_to, "N": near_to, "T": terms}
        for stage, k in PLAN:
            stages[stage](k)

    def gather(v, blocks):
        places = []
        for w in range(4):
            code, owner = owner_of(2 * v + w // 2)
            row = jnp.maximum(row_ref[w % 2, owner], 0)
            block = jnp.maximum(col_ref[w % 2, owner], 0) // 128
            places.append((row, block))
        picks = [
            [
                [
                    jnp.where((b - block >= 0) & (b - block < 3), w * 6 + p * 3 + b - block, 24)
                    for w, (row, block) in enumerate(places)
                ]
                for b in range(6)
            ]
            for p in range(2)
        ]

        def rows_of(ic, c):
            rows = pl.ds(pl.multiple_of(ic * CH, CH), CH)
            starts = [jnp.clip(ic * CH - row, -RP, 256) + RP for row, block in places]
            for b in blocks:
                for p in range(2):
                    acc = grad[p, b, rows, :]
                    for w in range(4):
                        acc = acc + term[picks[p][b][w], pl.ds(starts[w], CH), :]
                    grad[p, b, rows, :] = acc
            return c

        lax.fori_loop(0, 768 // CH, rows_of, 0)

    def sib_copy(i):
        return remote(sib_s.at[i], sib_r.at[i], sib_ss.at[i], sib_rs.at[i], {"obj": 2 * yy + 1 - core})

    def y_copy(i, d):
        to = (yy + d) % 4
        return remote(
            y_s.at[i, to], y_r.at[i, d - 1], y_ss.at[i * 3 + d - 1], y_rs.at[i * 3 + d - 1], {"obj": 2 * to + core}
        )

    def q_copy(i, a):
        code, owner = owner_of(2 * i + a)
        return remote(q_s.at[i, a], q_r.at[code], q_ss.at[code], q_rs.at[code], {"scan": owner // 4 * 4 + x})

    mine = pl.ds(pl.multiple_of(core * 128, 128), 128)
    other = pl.ds(pl.multiple_of((1 - core) * 128, 128), 128)

    def sib_stage(i):
        for a in range(2):
            for p in range(2):
                sib_s[i, a, p] = pacc[a, p, other, :].astype(BF16)
                kept[i % 2, a, p] = pacc[a, p, mine, :]
        sib_copy(i).start()

    def y_stage(i):
        sib_copy(i).wait_recv()
        for a in range(2):
            for p in range(2):
                total = kept[i % 2, a, p] + sib_r[i, a, p].astype(F32)
                for q in range(4):
                    y_s[i, q, a, p] = total[q * 32 : q * 32 + 32].astype(BF16)
        for d in range(1, 4):
            y_copy(i, d).start()

    def q_stage(i):
        for d in range(1, 4):
            y_copy(i, d).wait_recv()
        for a in range(2):
            for p in range(2):
                total = y_s[i, yy, a, p].astype(F32)
                for d in range(3):
                    total = total + y_r[i, d, a, p].astype(F32)
                q_s[i, a, p] = total.astype(BF16)

        for a in range(2):
            code, owner = owner_of(2 * i + a)

            @pl.when(code >= 4)
            def _():
                q_copy(i, a).start()

            @pl.when(code < 4)
            def _():
                q_r[code] = q_s[i, a]

    def step(v, c):
        @pl.when(v >= 1)
        def _():
            y_stage(v - 1)

        @pl.when(v >= 2)
        def _():
            q_stage(v - 2)

        four(v)
        sib_stage(v)
        gather(v, (4, 5))

        @pl.when(v < 7)
        def _():
            gather(v, (0, 1, 2, 3))

        return c

    lax.fori_loop(0, 8, step, 0)

    def z_wait(code):
        remote(q_s.at[0, 0], q_r.at[code], q_ss.at[code], q_rs.at[code], {"scan": right}).wait_recv()

    def x_copy(dx):
        return remote(x_s.at[dx], x_r.at[dx], x_ss.at[dx], x_rs.at[dx], {"scan": z * 4 + (x + 4 - dx) % 4})

    def x_stage(dx):
        for dz in range(1, 4):
            z_wait(dz * 4 + dx)
        for p in range(2):
            total = q_r[dx, p].astype(F32)
            for dz in range(1, 4):
                total = total + q_r[dz * 4 + dx, p].astype(F32)
            x_s[dx, p] = total.astype(BF16)
        x_copy(dx).start()

    x_stage(1)

    def rim_low_half(i, c):
        rows = pl.ds(pl.multiple_of(i * 64, 64), 64)
        src = pl.ds(pl.multiple_of(256 + i * 64, 64), 64)
        for p in range(2):
            for b in range(2):
                rim_s[1, p, b, rows, :] = grad[p, 4 + b, src, :].astype(BF16)
        return c

    lax.fori_loop(0, 4, rim_low_half, 0)
    rim_b = remote(rim_s.at[1], rim_r.at[1], rim_ss.at[1], rim_rs.at[1], {"scan": right})
    rim_b.start()
    y_stage(7)

    def corner_out(i, c):
        rows = pl.ds(pl.multiple_of(i * 64, 64), 64)
        low = pl.ds(pl.multiple_of(512 + i * 64, 64), 64)
        for p in range(2):
            for b in range(2):
                lrim_s[0, p, b, rows, :] = grad[p, 4 + b, low, :].astype(BF16)
        return c

    lax.fori_loop(0, 4, corner_out, 0)
    crim_cp = remote(lrim_s.at[0], crim_r, rim_ss.at[0], rim_rs.at[0], {"obj": below})
    crim_cp.start()
    q_stage(6)
    gather(7, (0, 1, 2, 3))

    def low_out(i, c):
        rows = pl.ds(pl.multiple_of(i * 64, 64), 64)
        low = pl.ds(pl.multiple_of(512 + i * 64, 64), 64)
        for p in range(2):
            for b in range(4):
                lrim_s[1 + b // 2, p, b % 2, rows, :] = grad[p, b, low, :].astype(BF16)
        return c

    lax.fori_loop(0, 4, low_out, 0)
    lrim_cp = remote(lrim_s.at[pl.ds(1, 2)], lrim_r, rim_ss.at[2], rim_rs.at[2], {"obj": below})
    lrim_cp.start()
    out_cps = []
    for p in range(2):
        for b in range(4):
            cp = pltpu.make_async_copy(
                grad.at[p, b, pl.ds(0, 512)], out.at[p, :, pl.ds(b * 128, 128)], local_sem.at[p * 4 + b]
            )
            cp.start()
            out_cps.append(cp)
    crim_cp.wait_recv()

    def rim_top_half(i, c):
        rows = pl.ds(pl.multiple_of(i * 64, 64), 64)
        for p in range(2):
            for b in range(2):
                rim_s[0, p, b, rows, :] = (grad[p, 4 + b, rows, :] + crim_r[p, b, rows, :].astype(F32)).astype(BF16)
        return c

    lax.fori_loop(0, 4, rim_top_half, 0)
    rim_t = remote(rim_s.at[0], rim_r.at[0], rim_ss.at[3], rim_rs.at[3], {"scan": right})
    rim_t.start()
    q_stage(7)

    x_stage(3)
    x_stage(2)
    for dz in range(1, 4):
        z_wait(dz * 4)
    for dx in range(1, 4):
        x_copy(dx).wait_recv()
    piece = core * 4 + yy
    for p in range(2):
        total = q_r[0, p].astype(F32)
        for dz in range(1, 4):
            total = total + q_r[dz * 4, p].astype(F32)
        for dx in range(1, 4):
            total = total + x_r[dx, p].astype(F32)
        g_s[p] = (total * (1.0 / 16.0)).astype(BF16)

    def g_copy(d):
        return remote(g_s, g_r.at[piece], g_ss.at[d - 1], g_rs.at[d - 1], {"obj": (band + d) % 8})

    for d in range(1, 8):
        g_copy(d).start()
    own_g = pltpu.make_async_copy(g_s, g_r.at[piece], local_sem.at[8])
    own_g.start()
    for d in range(1, 8):
        frm = (band + 8 - d) % 8
        at = frm % 2 * 4 + frm // 2
        remote(g_s, g_r.at[at], g_ss.at[d - 1], g_rs.at[d - 1], {"obj": frm}).wait_recv()
    for cp in (lrim_cp, rim_b, rim_t):
        cp.wait_recv()

    for cp in (*strip_cps, low_cp, corner_cp, crim_cp, rim_b, lrim_cp, rim_t):
        cp.wait_send()
    for t, s in sends:
        amp_copy(t, s).wait_send()

    def drain(i, c):
        sib_copy(i).wait_send()
        for d in range(1, 4):
            y_copy(i, d).wait_send()

        for a in range(2):

            @pl.when(owner_of(2 * i + a)[0] >= 4)
            def _():
                q_copy(i, a).wait_send()
        return c

    lax.fori_loop(0, 8, drain, 0)
    for d in range(1, 8):
        g_copy(d).wait_send()
    for dx in range(1, 4):
        x_copy(dx).wait_send()
    own_g.wait()
    for cp in out_cps:
        cp.wait()


def finish_kernel(main, rim, low, pieces, out, pout):
    out[...] = main[...]
    for b in range(2):
        for h in range(2):
            at = (0, slice(h * 256, h * 256 + 256), slice(b * 128, b * 128 + 128))
            out[at] = out[at] + rim[h, 0, b].astype(F32)
    for b in range(4):
        at = (0, slice(0, 256), slice(b * 128, b * 128 + 128))
        out[at] = out[at] + low[b // 2, 0, b % 2].astype(F32)
    for q in range(8):
        pout[0, 0, q * 32 : q * 32 + 32, :] = pieces[q, 0].astype(F32)


def on_device(object_field, probe, amplitudes, corner_row, corner_col):
    ltab, rtab = dft_tables(256)
    vm = pltpu.VMEM
    dma = pltpu.SemaphoreType.DMA
    anywhere = pl.BlockSpec(memory_space=pl.ANY)
    inside = pl.BlockSpec(memory_space=pltpu.VMEM)
    scalar = pl.BlockSpec(memory_space=pltpu.SMEM)
    main, rim, low, pieces = pl.pallas_call(
        kernel,
        out_shape=(
            jax.ShapeDtypeStruct((2, 512, 512), F32),
            jax.ShapeDtypeStruct((2, 2, 2, 256, 128), BF16),
            jax.ShapeDtypeStruct((2, 2, 2, 256, 128), BF16),
            jax.ShapeDtypeStruct((8, 2, 32, 256), BF16),
        ),
        in_specs=[scalar, scalar, anywhere, inside, anywhere, inside, inside],
        out_specs=(anywhere,) * 4,
        scratch_shapes=[
            vm((32, 256, 256), BF16),
            vm((2, 9, 768, 128), F32),
            vm((2, 6, 768, 128), F32),
            vm((25, 256 + 2 * RP, 128), F32),
            vm((4, 2, 256, 256), BF16),
            vm((4, 512, 256), BF16),
            vm((4, 256, 512), BF16),
            vm((4, 512, 256), BF16),
            vm((4, 256, 512), BF16),
            vm((8, 256, 512), F32),
            vm((2, 2, 256, 256), F32),
            vm((2, 2, 2, 256, 128), BF16),
            vm((2, 2, 2, 256, 128), BF16),
            vm((2, 4, 256, 128), BF16),
            vm((2, 4, 256, 128), BF16),
            vm((2, 2, 256, 128), BF16),
            vm((8, 2, 2, 128, 256), BF16),
            vm((8, 2, 2, 128, 256), BF16),
            vm((2, 2, 2, 128, 256), F32),
            vm((8, 4, 2, 2, 32, 256), BF16),
            vm((8, 3, 2, 2, 32, 256), BF16),
            vm((8, 2, 2, 32, 256), BF16),
            vm((16, 2, 32, 256), BF16),
            vm((4, 2, 32, 256), BF16),
            vm((4, 2, 32, 256), BF16),
            vm((2, 32, 256), BF16),
            vm((2, 2, 2, 256, 128), BF16),
            vm((3, 2, 2, 256, 128), BF16),
            vm((2, 2, 256, 128), BF16),
            dma((10,)),
            dma((4,)), dma((4,)),
            dma((32,)), dma((32,)),
            dma((8,)), dma((8,)),
            dma((24,)), dma((24,)),
            dma((16,)), dma((16,)),
            dma((4,)), dma((4,)),
            dma((7,)), dma((7,)),
            dma((4,)), dma((4,)),
        ],
        compiler_params=pltpu.CompilerParams(
            collective_id=0, has_side_effects=True, vmem_limit_bytes=62 * 2**20
        ),
        cost_estimate=pl.CostEstimate(flops=32 * 16 * 2 * 256**3, bytes_accessed=10 * 2**20, transcendentals=32 * 65536),
    )(
        corner_row[0].T, corner_col[0].T, object_field, probe, amplitudes[0],
        jnp.asarray(ltab), jnp.asarray(rtab),
    )
    return tuple(
        pl.pallas_call(
            finish_kernel,
            grid=(2,),
            in_specs=[
                pl.BlockSpec((1, 512, 512), lambda p: (p, 0, 0)),
                pl.BlockSpec((2, 1, 2, 256, 128), lambda p: (0, p, 0, 0, 0)),
                pl.BlockSpec((2, 1, 2, 256, 128), lambda p: (0, p, 0, 0, 0)),
                pl.BlockSpec((8, 1, 32, 256), lambda p: (0, p, 0, 0)),
            ],
            out_specs=(
                pl.BlockSpec((1, 512, 512), lambda p: (p, 0, 0)),
                pl.BlockSpec((1, 1, 256, 256), lambda p: (0, p, 0, 0)),
            ),
            out_shape=(
                jax.ShapeDtypeStruct((2, 512, 512), F32),
                jax.ShapeDtypeStruct((1, 2, 256, 256), F32),
            ),
            compiler_params=pltpu.CompilerParams(vmem_limit_bytes=60 * 2**20),
        )(main, rim, low, pieces)
    )


def solution(mesh):
    return jax.shard_map(
        on_device,
        mesh=mesh,
        in_specs=(
            P(None, "obj", "scan"),
            P(),
            P("obj", "scan", None, None),
            P("obj", "scan", None),
            P("obj", "scan", None),
        ),
        out_specs=(P(None, "obj", "scan"), P("scan", None, None, None)),
        check_vma=False,
    )
```
